512 devices in a mesh: grp: 4 (over z_lo, core), slab: 128 (over y, x, z_hi).
Axes of the slice: x: 4, y: 8, z: 8 (z_hi: 4, z_lo: 2; z = z_hi * 2 + z_lo), core: 2. Of those that a mesh axis runs over, the one named last changes fastest.
Arguments:
- theta: float32 [4, 2048, 64, 256], P('grp', 'slab'), may hold values from -6 to 6
- register: float32 [4, 2048, 64, 256], P('grp', 'slab'), may hold values from -6 to 6
- velocity: bfloat16 [3, 1024, 32, 128], P(None, 'slab', 'grp'), may hold values from -6 to 6
- diffusivity: float32 [4], P('grp'), may hold values from 0.05 to 0.5
Outputs:
- theta_new: float32 [4, 2048, 64, 256], P('grp', 'slab')
- register_new: float32 [4, 2048, 64, 256], P('grp', 'slab')
The draws below stay inside these ranges and needn't reach their ends.
All inputs are finite; a program needn't handle non-finite values.
Results may differ from the reference program's by a relative error of at most 0.0014.
Values may be sent and summed in bfloat16 or wider, within the bound.
A program may use at most 64 MiB of HBM per device.

```python
import math
import jax
import jax.numpy as jnp
from jax import lax

PX = 16
BLK = 32
NYF = 64
NZF = 256
NXF = 2048
NXC = 1024
NYC = 32
NZC = 128
SCALARS = 4


def block_levels(own_key, shape, cuts, smallest, largest):
    gain, own = 1.0, jax.random.fold_in(own_key, 6)
    for axis_at, parts in cuts:
        heights = jnp.exp(jax.random.uniform(jax.random.fold_in(own, axis_at), (parts,), jnp.float32, smallest / len(cuts), largest / len(cuts)))
        gain = gain * jnp.repeat(heights, shape[axis_at] // parts).reshape([-1 if axis == axis_at else 1 for axis in range(len(shape))])
    return gain


def noise(stream_key, dims, width, limit, cuts=(), kind=jnp.bfloat16):
    drawn = jax.random.normal(stream_key, dims, jnp.float32) * width
    if len(cuts) > 0:
        drawn = block_levels(stream_key, dims, cuts, -0.22, 0.18) * drawn
    return jnp.clip(drawn, min=-limit, max=limit).astype(kind)


def setup_inputs(seed: int = 0) -> dict:
    arg_keys = jax.random.split(jax.random.key(seed), 5)
    return {
        "theta": noise(arg_keys[0], (SCALARS, NXF, NYF, NZF), 1.0, 6.0, ((0, 4), (1, 128)), jnp.float32),
        "register": noise(arg_keys[1], (SCALARS, NXF, NYF, NZF), 1.0, 6.0, ((0, 4), (1, 128)), jnp.float32),
        "velocity": noise(arg_keys[2], (3, NXC, NYC, NZC), 1.0, 6.0, ((1, 128), (2, 4))),
        "diffusivity": jnp.clip(jnp.exp(math.log(0.5) - 2.3025851 * jax.random.uniform(arg_keys[3], (SCALARS,), jnp.float32) ** block_levels(arg_keys[3], (SCALARS,), ((0, 4),), -0.2, 0.2)), 0.05, 0.5),
    }


ALPHA = 4.0 / 9.0
BETA = 1.0 / 36.0
COEF_A = 40.0 / 27.0
COEF_B = 25.0 / 54.0
RK_A = -5.0 / 9.0
RK_B = 15.0 / 16.0
STEP = 0.2

def band_matrices(count, periodic):
    rows = jnp.arange(count)[:, None]
    cols = jnp.arange(count)[None, :]
    offset = cols - rows
    if periodic:
        offset = (offset + count // 2) % count - count // 2
    one = jnp.float32(1.0)
    zero = jnp.float32(0.0)
    lhs = jnp.where(offset == 0, one, zero) + ALPHA * jnp.where(jnp.abs(offset) == 1, one, zero) + BETA * jnp.where(jnp.abs(offset) == 2, one, zero)
    rhs = 0.5 * COEF_A * (jnp.where(offset == 1, one, zero) - jnp.where(offset == -1, one, zero)) + 0.25 * COEF_B * (jnp.where(offset == 2, one, zero) - jnp.where(offset == -2, one, zero))
    return (lhs, rhs)

def block_inverse(count):
    lhs, rhs = band_matrices(count, False)
    factor = jnp.linalg.cholesky(lhs)
    return jax.scipy.linalg.cho_solve((factor, True), jnp.eye(count, dtype=lhs.dtype))

def blocked_operator(count, block):
    lhs, rhs = band_matrices(count, True)
    inverse = block_inverse(block)
    diagonal = jnp.kron(jnp.eye(count // block, dtype=jnp.float32), inverse)
    return jnp.dot(diagonal, rhs, precision=lax.Precision.HIGHEST)

def wrap_pad(field, axis):
    count = field.shape[axis]
    left = lax.slice_in_dim(field, count - 2, count, axis=axis)
    right = lax.slice_in_dim(field, 0, 2, axis=axis)
    return jnp.concatenate([left, field, right], axis=axis)

def refine(padded, axis, count):

    def taken(shift):
        return lax.slice_in_dim(padded, 2 + shift, 2 + shift + count, axis=axis)
    even = -0.0390625 * taken(-2) + 0.2734375 * taken(-1) + 0.8203125 * taken(0) - 0.0546875 * taken(1)
    odd = -0.0546875 * taken(-1) + 0.8203125 * taken(0) + 0.2734375 * taken(1) - 0.0390625 * taken(2)
    stacked = jnp.stack([even, odd], axis=axis + 1)
    shape = list(even.shape)
    shape[axis] = 2 * count
    return stacked.reshape(shape)

def x_derivative(field, inverse):
    rhs = 0.5 * COEF_A * (jnp.roll(field, -1, 0) - jnp.roll(field, 1, 0)) + 0.25 * COEF_B * (jnp.roll(field, -2, 0) - jnp.roll(field, 2, 0))
    blocks = rhs.reshape((-1, PX) + field.shape[1:])
    out = jnp.einsum('ij,bjyz->biyz', inverse, blocks, precision=lax.Precision.HIGHEST)
    return out.reshape(field.shape)

def y_derivative(field, operator):
    return jnp.einsum('ij,xjz->xiz', operator, field, precision=lax.Precision.HIGHEST)

def z_derivative(field, operator):
    return jnp.einsum('ij,xyj->xyi', operator, field, precision=lax.Precision.HIGHEST)

def reference(theta, register, velocity, diffusivity):
    coarse = velocity.astype(jnp.float32)
    flow = refine(wrap_pad(coarse, 1), 1, coarse.shape[1])
    flow = refine(wrap_pad(flow, 2), 2, flow.shape[2])
    flow = refine(wrap_pad(flow, 3), 3, flow.shape[3])
    inverse = block_inverse(PX)
    oper_y = blocked_operator(NYF, BLK)
    oper_z = blocked_operator(NZF, BLK)

    def one_scalar(items):
        field, saved, kappa = items
        grad_x = x_derivative(field, inverse)
        grad_y = y_derivative(field, oper_y)
        grad_z = z_derivative(field, oper_z)
        flux_x = flow[0] * field - kappa * grad_x
        flux_y = flow[1] * field - kappa * grad_y
        flux_z = flow[2] * field - kappa * grad_z
        rate = -(x_derivative(flux_x, inverse) + y_derivative(flux_y, oper_y) + z_derivative(flux_z, oper_z))
        new_saved = RK_A * saved + STEP * rate
        return (field + RK_B * new_saved, new_saved)
    theta_new, register_new = lax.map(one_scalar, (theta, register, diffusivity))
    return (theta_new, register_new)
```

```python
import jax
import jax.numpy as jnp
import numpy as np
from jax import lax
from jax.experimental import pallas as pl
from jax.experimental.pallas import tpu as pltpu
from jax.sharding import PartitionSpec as P

PX = 16
BLK = 32
NYF = 64
NZF = 256
ALPHA = 4.0 / 9.0
BETA = 1.0 / 36.0
COEF_A = 40.0 / 27.0
COEF_B = 25.0 / 54.0
RK_A = -5.0 / 9.0
RK_B = 15.0 / 16.0
STEP = 0.2
CHUNKS = 4
ROWS = NYF // CHUNKS
MESH = pl.DeviceIdType.MESH
F32 = jnp.float32
BF16 = jnp.bfloat16


def band(count):
    eye = lambda k: np.eye(count, k=k)
    return eye(0) + ALPHA * (eye(1) + eye(-1)) + BETA * (eye(2) + eye(-2))


def periodic_rhs(count):
    out = np.zeros((count, count))
    for i in range(count):
        for shift, weight in ((1, 0.5 * COEF_A), (2, 0.25 * COEF_B)):
            out[i, (i + shift) % count] += weight
            out[i, (i - shift) % count] -= weight
    return out


def blocked_operator(count):
    inverse = np.linalg.inv(band(BLK))
    return np.kron(np.eye(count // BLK), inverse) @ periodic_rhs(count)


def refine_matrix(count):
    out = np.zeros((2 * count, count))
    for k in range(count):
        for shift, even, odd in (
            (-2, -0.0390625, 0.0),
            (-1, 0.2734375, -0.0546875),
            (0, 0.8203125, 0.8203125),
            (1, -0.0546875, 0.2734375),
            (2, 0.0, -0.0390625),
        ):
            out[2 * k, (k + shift) % count] += even
            out[2 * k + 1, (k + shift) % count] += odd
    return out


def split_constant(matrix):
    high = jnp.asarray(matrix, F32).astype(BF16)
    rest = matrix - np.asarray(high.astype(F32), np.float64)
    return np.asarray(high), np.asarray(jnp.asarray(rest, F32).astype(BF16))


def constants():
    dz = split_constant(blocked_operator(NZF).T)
    dy = split_constant(np.kron(np.eye(4), blocked_operator(NYF)))
    ry = np.kron(np.eye(4), refine_matrix(NYF // 2))
    ry = split_constant(np.concatenate([ry, ry], axis=1))[0]
    rz = refine_matrix(NZF // 2).T
    rz = split_constant(np.concatenate([rz, rz], axis=0))[0]
    return np.stack([dz[0], dz[1], dy[0], dy[1], ry, rz])


def halo_weights():
    inverse = np.linalg.inv(band(PX))
    first, second = 0.5 * COEF_A, 0.25 * COEF_B
    return np.stack(
        [
            -second * inverse[:, 0],
            -first * inverse[:, 0] - second * inverse[:, 1],
            second * inverse[:, PX - 2] + first * inverse[:, PX - 1],
            second * inverse[:, PX - 1],
        ],
        axis=1,
    )


def factors():
    lower1, lower2, diag = np.zeros(PX), np.zeros(PX), np.zeros(PX)
    for i in range(PX):
        if i >= 2:
            lower2[i] = BETA / diag[i - 2]
        if i >= 1:
            off = ALPHA - (lower2[i] * diag[i - 2] * lower1[i - 1] if i >= 2 else 0.0)
            lower1[i] = off / diag[i - 1]
        diag[i] = (
            1.0
            - (lower1[i] ** 2 * diag[i - 1] if i >= 1 else 0.0)
            - (lower2[i] ** 2 * diag[i - 2] if i >= 2 else 0.0)
        )
    return lower1, lower2, diag


WEIGHTS = halo_weights()
LOWER1, LOWER2, DIAG = factors()


def x_local(planes):
    ratio = 0.25 * COEF_B / (0.5 * COEF_A)
    scale = 0.5 * COEF_A

    def diff(i, shift):
        ahead, behind = i + shift, i - shift
        if ahead >= PX:
            return -planes[behind]
        if behind < 0:
            return planes[ahead]
        return planes[ahead] - planes[behind]

    out = []
    for i in range(PX):
        value = diff(i, 1) + ratio * diff(i, 2)
        if i >= 1:
            value = value - float(LOWER1[i]) * out[i - 1]
        if i >= 2:
            value = value - float(LOWER2[i]) * out[i - 2]
        out.append(value)
    for i in reversed(range(PX)):
        value = float(scale / DIAG[i]) * out[i]
        if i + 1 < PX:
            value = value - float(LOWER1[i + 1]) * out[i + 1]
        if i + 2 < PX:
            value = value - float(LOWER2[i + 2]) * out[i + 2]
        out[i] = value
    return out


def halo_term(halo, i, factor=1.0):
    total = float(factor * WEIGHTS[i, 0]) * halo[0]
    for k in range(1, 4):
        total = total + float(factor * WEIGHTS[i, k]) * halo[k]
    return total


def split(value):
    high = value.astype(BF16)
    return high, (value - high.astype(F32)).astype(BF16)


def mm(left, right):
    return jnp.dot(left, right, preferred_element_type=F32)


def kernel(
    theta, register, velocity, kappa, consts, out_field, out_saved,
    th, reg, mat, vel, grad, grad_y, grad_z, flow_x,
    send_t, recv_t, send_f, recv_f,
    load_sem, v_send, v_recv, t_send, t_recv, f_send, f_recv,
):
    grp, slab = lax.axis_index("grp"), lax.axis_index("slab")
    count = lax.axis_size("slab")
    right, left = lax.rem(slab + 1, count), lax.rem(slab + count - 1, count)
    peer = lax.rem(grp + 2, 4)
    mate = grp + 1 - 2 * lax.rem(grp, 2)

    def load(src, dst, k):
        copy = pltpu.make_async_copy(src, dst, load_sem.at[k])
        copy.start()
        return copy

    edges = [
        load(theta.at[pl.ds(0, 2)], th.at[pl.ds(0, 2)], 0),
        load(theta.at[pl.ds(PX - 2, 2)], th.at[pl.ds(PX - 2, 2)], 1),
    ]
    own_vel = load(velocity, vel.at[grp, :, pl.ds(16, 64)], 2)
    inner = load(theta.at[pl.ds(2, PX - 4)], th.at[pl.ds(2, PX - 4)], 3)
    load_mat = load(consts, mat, 4)
    load_reg = load(register, reg, 5)

    barrier = pltpu.get_barrier_semaphore()
    partners = [
        {"grp": peer, "slab": slab},
        {"grp": mate, "slab": slab},
        {"grp": grp, "slab": right},
        {"grp": peer, "slab": right},
        {"grp": grp, "slab": left},
        {"grp": peer, "slab": left},
    ]
    for partner in partners:
        pl.semaphore_signal(barrier, inc=1, device_id=partner, device_id_type=MESH)
    pl.semaphore_wait(barrier, len(partners))

    def remote(src, dst, send_sem, recv_sem, device):
        copy = pltpu.make_async_remote_copy(
            src_ref=src, dst_ref=dst, send_sem=send_sem, recv_sem=recv_sem,
            device_id=device, device_id_type=MESH,
        )
        copy.start()
        return copy

    def velocity_sends(part, first, width):
        comps = pl.ds(first, width)

        def sent(rows, to_rows, size, k, device):
            return remote(
                velocity.at[comps, pl.ds(rows, size)],
                vel.at[grp, comps, pl.ds(to_rows, size)],
                v_send.at[part, k], v_recv.at[part, k], device,
            )

        return [
            sent(0, 16, 64, 0, partners[0]),
            sent(48, 0, 16, 1, partners[2]),
            sent(0, 80, 16, 2, partners[4]),
            sent(48, 0, 16, 3, partners[3]),
            sent(0, 80, 16, 4, partners[5]),
        ]

    def velocity_forward(part, first, width, sends):
        for copy in sends:
            copy.wait_recv()
        comps = pl.ds(first, width)
        return [
            remote(
                vel.at[quarter, comps], vel.at[quarter, comps],
                v_send.at[part, 5 + k], v_recv.at[part, 5 + k], partners[1],
            )
            for k, quarter in enumerate((grp, peer))
        ]

    vel_first = velocity_sends(0, 0, 1)

    for copy in edges:
        copy.wait()
    theta_sends = []
    for c in range(CHUNKS):
        rows = pl.ds(c * ROWS, ROWS)
        for side, (first, device) in enumerate(((PX - 2, partners[2]), (0, partners[4]))):
            send_t[side, c] = th[pl.ds(first, 2), rows, :].astype(BF16)
            theta_sends.append(
                remote(
                    send_t.at[side, c], recv_t.at[side, c],
                    t_send.at[side, c], t_recv.at[side, c], device,
                )
            )

    vel_rest = velocity_sends(1, 1, 2)

    inner.wait()

    @pl.loop(0, NYF // 8)
    def _(t):
        rows = pl.ds(pl.multiple_of(t * 8, 8), 8)
        out = x_local([th[p, rows, :] for p in range(PX)])
        for p in range(PX):
            grad[p, rows, :] = out[p]

    own_vel.wait()
    vel_first_forward = velocity_forward(0, 0, 1, vel_first)

    load_mat.wait()
    kap = kappa[0]

    @pl.loop(0, PX // 4)
    def _(j):
        planes = pl.ds(j * 4, 4)
        high, low = split(th[planes].reshape(4 * NYF, NZF))
        value = mm(mat[2], high) + mm(mat[2], low) + mm(mat[3], high)
        grad_y[planes] = (kap * value).reshape(4, NYF, NZF)
        value = mm(high, mat[0]) + mm(low, mat[0]) + mm(high, mat[1])
        grad_z[planes] = (kap * value).reshape(4, NYF, NZF)

    def flow(comp, j):
        tiles = []
        for quarter in range(4):
            rows = pl.ds(pl.multiple_of(16 * j, 16), 48)
            coarse = vel[quarter, comp, rows, :].astype(F32).reshape(6, 8, NZF // 2)
            fine = []
            for k in range(2):
                fine.append(
                    -0.0390625 * coarse[k] + 0.2734375 * coarse[k + 1]
                    + 0.8203125 * coarse[k + 2] - 0.0546875 * coarse[k + 3]
                )
                fine.append(
                    -0.0546875 * coarse[k + 1] + 0.8203125 * coarse[k + 2]
                    + 0.2734375 * coarse[k + 3] - 0.0390625 * coarse[k + 4]
                )
            tiles.append(fine)
        stacked = jnp.concatenate(
            [tiles[quarter][p] for p in range(4) for quarter in range(4)], axis=0
        )
        wide = mm(mat[4], jnp.concatenate(split(stacked), axis=0))
        return mm(jnp.concatenate(split(wide), axis=1), mat[5])

    for copy in vel_first_forward:
        copy.wait_recv()

    @pl.loop(0, PX // 4)
    def _(j):
        flow_x[pl.ds(j * 4, 4)] = flow(0, j).reshape(4, NYF, NZF)

    def halo_of(buffer, c, rows):
        return [
            buffer[0, c, 0, rows, :].astype(F32),
            buffer[0, c, 1, rows, :].astype(F32),
            buffer[1, c, 0, rows, :].astype(F32),
            buffer[1, c, 1, rows, :].astype(F32),
        ]

    flux_sends = []
    for c in range(CHUNKS):
        for side in range(2):
            theta_sends[2 * c + side].wait_recv()
        rows = pl.ds(c * ROWS, ROWS)
        halo = halo_of(recv_t, c, pl.ds(0, ROWS))
        for side, (first, device) in enumerate(((PX - 2, partners[2]), (0, partners[4]))):
            for k in range(2):
                p = first + k
                value = grad[p, rows, :] + halo_term(halo, p)
                flux = flow_x[p, rows, :] * th[p, rows, :] - kap * value
                send_f[side, c, k] = flux.astype(BF16)
            flux_sends.append(
                remote(
                    send_f.at[side, c], recv_f.at[side, c],
                    f_send.at[side, c], f_recv.at[side, c], device,
                )
            )

    vel_rest_forward = velocity_forward(1, 1, 2, vel_rest)

    load_reg.wait()

    @pl.loop(0, CHUNKS)
    def _(c):
        halo = halo_of(recv_t, c, pl.ds(0, ROWS))
        for part in range(ROWS // 8):
            rows = pl.ds(pl.multiple_of(c * ROWS + part * 8, 8), 8)
            near = [h[part * 8 : part * 8 + 8] for h in halo]
            planes = []
            for p in range(PX):
                value = grad[p, rows, :] + halo_term(near, p)
                planes.append(flow_x[p, rows, :] * th[p, rows, :] - kap * value)
            out = x_local(planes)
            for p in range(PX):
                grad[p, rows, :] = RK_A * reg[p, rows, :] - STEP * out[p]

    for copy in vel_rest_forward:
        copy.wait_recv()

    @pl.loop(0, PX // 4)
    def _(j):
        planes = pl.ds(j * 4, 4)
        field = th[planes].reshape(4 * NYF, NZF)
        flux = flow(1, j) * field - grad_y[planes].reshape(4 * NYF, NZF)
        high, low = split(flux)
        total = mm(mat[2], high) + mm(mat[2], low) + mm(mat[3], high)
        flux = flow(2, j) * field - grad_z[planes].reshape(4 * NYF, NZF)
        high, low = split(flux)
        total = total + mm(high, mat[0]) + mm(low, mat[0]) + mm(high, mat[1])
        grad[planes] = grad[planes] - STEP * total.reshape(4, NYF, NZF)

    for c in range(CHUNKS):
        for side in range(2):
            flux_sends[2 * c + side].wait_recv()
        rows = pl.ds(c * ROWS, ROWS)
        halo = halo_of(recv_f, c, pl.ds(0, ROWS))
        for p in range(PX):
            saved = grad[p, rows, :] + halo_term(halo, p, -STEP)
            out_saved[p, rows, :] = saved
            out_field[p, rows, :] = th[p, rows, :] + RK_B * saved

    for copy in vel_first + vel_rest + vel_first_forward + vel_rest_forward:
        copy.wait_send()
    for copy in theta_sends + flux_sends:
        copy.wait_send()


def solution(mesh):
    table = constants()
    block = (PX, NYF, NZF)
    whole = jax.ShapeDtypeStruct(block, F32)
    hbm = pl.BlockSpec(memory_space=pltpu.HBM)
    halo = pltpu.VMEM((2, CHUNKS, 2, ROWS, NZF), BF16)
    call = pl.pallas_call(
        kernel,
        out_shape=(whole, whole),
        in_specs=[hbm, hbm, hbm, pl.BlockSpec(memory_space=pltpu.SMEM), hbm],
        out_specs=[pl.BlockSpec(memory_space=pltpu.VMEM)] * 2,
        scratch_shapes=[
            pltpu.VMEM(block, F32),
            pltpu.VMEM(block, F32),
            pltpu.VMEM((6, 256, 256), BF16),
            pltpu.VMEM((4, 3, 96, NZF // 2), BF16),
            pltpu.VMEM(block, F32),
            pltpu.VMEM(block, F32),
            pltpu.VMEM(block, F32),
            pltpu.VMEM(block, F32),
            halo, halo, halo, halo,
            pltpu.SemaphoreType.DMA((6,)),
            pltpu.SemaphoreType.DMA((2, 7)),
            pltpu.SemaphoreType.DMA((2, 7)),
            pltpu.SemaphoreType.DMA((2, CHUNKS)),
            pltpu.SemaphoreType.DMA((2, CHUNKS)),
            pltpu.SemaphoreType.DMA((2, CHUNKS)),
            pltpu.SemaphoreType.DMA((2, CHUNKS)),
        ],
        compiler_params=pltpu.CompilerParams(
            collective_id=0, has_side_effects=True, vmem_limit_bytes=24 * 2**20
        ),
    )

    def shards(theta, register, velocity, diffusivity):
        coarse = velocity.reshape(3, 64, NZF // 2)
        field, saved = call(
            theta.reshape(block), register.reshape(block), coarse, diffusivity, jnp.asarray(table)
        )
        return (field[None], saved[None])

    spec = P("grp", "slab", None, None)
    return jax.shard_map(
        shards, mesh=mesh,
        in_specs=(spec, spec, P(None, "slab", "grp", None), P("grp")),
        out_specs=(spec, spec), check_vma=False,
    )
```

```python
import jax
import jax.numpy as jnp
import numpy as np
from jax import lax
from jax.experimental import pallas as pl
from jax.experimental.pallas import tpu as pltpu
from jax.sharding import PartitionSpec as P

PX = 16
BLK = 32
NYF = 64
NZF = 256
ALPHA = 4.0 / 9.0
BETA = 1.0 / 36.0
COEF_A = 40.0 / 27.0
COEF_B = 25.0 / 54.0
RK_A = -5.0 / 9.0
RK_B = 15.0 / 16.0
STEP = 0.2
CHUNKS = 4
ROWS = NYF // CHUNKS
MESH = pl.DeviceIdType.MESH
F32 = jnp.float32
BF16 = jnp.bfloat16


def band(count):
    eye = lambda k: np.eye(count, k=k)
    return eye(0) + ALPHA * (eye(1) + eye(-1)) + BETA * (eye(2) + eye(-2))


def periodic_rhs(count):
    out = np.zeros((count, count))
    for i in range(count):
        for shift, weight in ((1, 0.5 * COEF_A), (2, 0.25 * COEF_B)):
            out[i, (i + shift) % count] += weight
            out[i, (i - shift) % count] -= weight
    return out


def blocked_operator(count):
    inverse = np.linalg.inv(band(BLK))
    return np.kron(np.eye(count // BLK), inverse) @ periodic_rhs(count)


def refine_matrix(count):
    out = np.zeros((2 * count, count))
    for k in range(count):
        for shift, even, odd in (
            (-2, -0.0390625, 0.0),
            (-1, 0.2734375, -0.0546875),
            (0, 0.8203125, 0.8203125),
            (1, -0.0546875, 0.2734375),
            (2, 0.0, -0.0390625),
        ):
            out[2 * k, (k + shift) % count] += even
            out[2 * k + 1, (k + shift) % count] += odd
    return out


def split_constant(matrix):
    high = jnp.asarray(matrix, F32).astype(BF16)
    rest = matrix - np.asarray(high.astype(F32), np.float64)
    return np.asarray(high), np.asarray(jnp.asarray(rest, F32).astype(BF16))


def constants():
    dz = split_constant(blocked_operator(NZF).T)
    dy = split_constant(np.kron(np.eye(4), blocked_operator(NYF)))
    ry = np.kron(np.eye(4), refine_matrix(NYF // 2))
    ry = split_constant(np.concatenate([ry, ry], axis=1))[0]
    rz = refine_matrix(NZF // 2).T
    rz = split_constant(np.concatenate([rz, rz], axis=0))[0]
    return np.stack([dz[0], dz[1], dy[0], dy[1], ry, rz])


def halo_weights():
    inverse = np.linalg.inv(band(PX))
    first, second = 0.5 * COEF_A, 0.25 * COEF_B
    return np.stack(
        [
            -second * inverse[:, 0],
            -first * inverse[:, 0] - second * inverse[:, 1],
            second * inverse[:, PX - 2] + first * inverse[:, PX - 1],
            second * inverse[:, PX - 1],
        ],
        axis=1,
    )


def factors():
    lower1, lower2, diag = np.zeros(PX), np.zeros(PX), np.zeros(PX)
    for i in range(PX):
        if i >= 2:
            lower2[i] = BETA / diag[i - 2]
        if i >= 1:
            off = ALPHA - (lower2[i] * diag[i - 2] * lower1[i - 1] if i >= 2 else 0.0)
            lower1[i] = off / diag[i - 1]
        diag[i] = (
            1.0
            - (lower1[i] ** 2 * diag[i - 1] if i >= 1 else 0.0)
            - (lower2[i] ** 2 * diag[i - 2] if i >= 2 else 0.0)
        )
    return lower1, lower2, diag


WEIGHTS = halo_weights()
LOWER1, LOWER2, DIAG = factors()


def x_local(planes):
    ratio = 0.25 * COEF_B / (0.5 * COEF_A)
    scale = 0.5 * COEF_A

    def diff(i, shift):
        ahead, behind = i + shift, i - shift
        if ahead >= PX:
            return -planes[behind]
        if behind < 0:
            return planes[ahead]
        return planes[ahead] - planes[behind]

    out = []
    for i in range(PX):
        value = diff(i, 1) + ratio * diff(i, 2)
        if i >= 1:
            value = value - float(LOWER1[i]) * out[i - 1]
        if i >= 2:
            value = value - float(LOWER2[i]) * out[i - 2]
        out.append(value)
    for i in reversed(range(PX)):
        value = float(scale / DIAG[i]) * out[i]
        if i + 1 < PX:
            value = value - float(LOWER1[i + 1]) * out[i + 1]
        if i + 2 < PX:
            value = value - float(LOWER2[i + 2]) * out[i + 2]
        out[i] = value
    return out


def halo_term(halo, i, factor=1.0):
    total = float(factor * WEIGHTS[i, 0]) * halo[0]
    for k in range(1, 4):
        total = total + float(factor * WEIGHTS[i, k]) * halo[k]
    return total


def split(value):
    high = value.astype(BF16)
    return high, (value - high.astype(F32)).astype(BF16)


def mm(left, right):
    return jnp.dot(left, right, preferred_element_type=F32)


def kernel(
    theta, register, velocity, kappa, consts, out_field, out_saved,
    th, reg, mat, vel, grad, grad_y, grad_z, flow_x,
    send_t, recv_t, send_f, recv_f,
    load_sem, v_send, v_recv, t_send, t_recv, f_send, f_recv,
):
    grp, slab = lax.axis_index("grp"), lax.axis_index("slab")
    count = lax.axis_size("slab")
    right, left = lax.rem(slab + 1, count), lax.rem(slab + count - 1, count)

    def load(src, dst, k):
        copy = pltpu.make_async_copy(src, dst, load_sem.at[k])
        copy.start()
        return copy

    def member(j):
        chip = lax.rem(lax.div(grp, 2) + j // 2, 2)
        core = lax.rem(lax.rem(grp, 2) + j % 2, 2)
        return 2 * chip + core

    spots = [(j, slab) for j in (1, 2, 3)] + [(j, s) for s in (right, left) for j in range(4)]
    partners = [{"grp": member(j), "slab": s} for j, s in spots]
    to_right, to_left = partners[3], partners[7]
    barrier = pltpu.get_barrier_semaphore()
    for partner in partners:
        pl.semaphore_signal(barrier, inc=1, device_id=partner, device_id_type=MESH)

    edges = [
        load(theta.at[pl.ds(0, 2)], th.at[pl.ds(0, 2)], 0),
        load(theta.at[pl.ds(PX - 2, 2)], th.at[pl.ds(PX - 2, 2)], 1),
    ]
    own_vel = load(velocity, vel.at[grp, :, pl.ds(16, 64)], 2)
    inner = load(theta.at[pl.ds(2, PX - 4)], th.at[pl.ds(2, PX - 4)], 3)
    load_mat = load(consts, mat, 4)
    load_reg = load(register, reg, 5)
    pl.semaphore_wait(barrier, len(partners))

    def remote(src, dst, send_sem, recv_sem, device):
        copy = pltpu.make_async_remote_copy(
            src_ref=src, dst_ref=dst, send_sem=send_sem, recv_sem=recv_sem,
            device_id=device, device_id_type=MESH,
        )
        copy.start()
        return copy

    vel_sends = []
    for k, partner in enumerate(partners):
        rows, to_rows, size = (0, 16, 64) if k < 3 else (48, 0, 16) if k < 7 else (0, 80, 16)
        vel_sends.append(
            remote(
                velocity.at[:, pl.ds(rows, size)], vel.at[grp, :, pl.ds(to_rows, size)],
                v_send.at[k], v_recv.at[k], partner,
            )
        )

    for copy in edges:
        copy.wait()
    theta_sends = []
    for c in range(CHUNKS):
        rows = pl.ds(c * ROWS, ROWS)
        for side, (first, device) in enumerate(((PX - 2, to_right), (0, to_left))):
            send_t[side, c] = th[pl.ds(first, 2), rows, :].astype(BF16)
            theta_sends.append(
                remote(
                    send_t.at[side, c], recv_t.at[side, c],
                    t_send.at[side, c], t_recv.at[side, c], device,
                )
            )

    inner.wait()

    @pl.loop(0, NYF // 8)
    def _(t):
        rows = pl.ds(pl.multiple_of(t * 8, 8), 8)
        out = x_local([th[p, rows, :] for p in range(PX)])
        for p in range(PX):
            grad[p, rows, :] = out[p]

    load_mat.wait()
    kap = kappa[0]

    @pl.loop(0, PX // 4)
    def _(j):
        planes = pl.ds(j * 4, 4)
        high, low = split(th[planes].reshape(4 * NYF, NZF))
        value = mm(mat[2], high) + mm(mat[2], low) + mm(mat[3], high)
        grad_y[planes] = (kap * value).reshape(4, NYF, NZF)
        value = mm(high, mat[0]) + mm(low, mat[0]) + mm(high, mat[1])
        grad_z[planes] = (kap * value).reshape(4, NYF, NZF)

    def flow(comp, j):
        tiles = []
        for quarter in range(4):
            rows = pl.ds(pl.multiple_of(16 * j, 16), 48)
            coarse = vel[quarter, comp, rows, :].astype(F32).reshape(6, 8, NZF // 2)
            fine = []
            for k in range(2):
                fine.append(
                    -0.0390625 * coarse[k] + 0.2734375 * coarse[k + 1]
                    + 0.8203125 * coarse[k + 2] - 0.0546875 * coarse[k + 3]
                )
                fine.append(
                    -0.0546875 * coarse[k + 1] + 0.8203125 * coarse[k + 2]
                    + 0.2734375 * coarse[k + 3] - 0.0390625 * coarse[k + 4]
                )
            tiles.append(fine)
        stacked = jnp.concatenate(
            [tiles[quarter][p] for p in range(4) for quarter in range(4)], axis=0
        )
        wide = mm(mat[4], jnp.concatenate(split(stacked), axis=0))
        return mm(jnp.concatenate(split(wide), axis=1), mat[5])

    own_vel.wait()
    for copy in vel_sends:
        copy.wait_recv()

    @pl.loop(0, PX // 4)
    def _(j):
        flow_x[pl.ds(j * 4, 4)] = flow(0, j).reshape(4, NYF, NZF)

    def halo_of(buffer, c, rows):
        return [
            buffer[0, c, 0, rows, :].astype(F32),
            buffer[0, c, 1, rows, :].astype(F32),
            buffer[1, c, 0, rows, :].astype(F32),
            buffer[1, c, 1, rows, :].astype(F32),
        ]

    flux_sends = []
    for c in range(CHUNKS):
        for side in range(2):
            theta_sends[2 * c + side].wait_recv()
        rows = pl.ds(c * ROWS, ROWS)
        halo = halo_of(recv_t, c, pl.ds(0, ROWS))
        for side, (first, device) in enumerate(((PX - 2, to_right), (0, to_left))):
            for k in range(2):
                p = first + k
                value = grad[p, rows, :] + halo_term(halo, p)
                flux = flow_x[p, rows, :] * th[p, rows, :] - kap * value
                send_f[side, c, k] = flux.astype(BF16)
            flux_sends.append(
                remote(
                    send_f.at[side, c], recv_f.at[side, c],
                    f_send.at[side, c], f_recv.at[side, c], device,
                )
            )

    load_reg.wait()

    @pl.loop(0, CHUNKS)
    def _(c):
        halo = halo_of(recv_t, c, pl.ds(0, ROWS))
        for part in range(ROWS // 8):
            rows = pl.ds(pl.multiple_of(c * ROWS + part * 8, 8), 8)
            near = [h[part * 8 : part * 8 + 8] for h in halo]
            planes = []
            for p in range(PX):
                value = grad[p, rows, :] + halo_term(near, p)
                planes.append(flow_x[p, rows, :] * th[p, rows, :] - kap * value)
            out = x_local(planes)
            for p in range(PX):
                grad[p, rows, :] = RK_A * reg[p, rows, :] - STEP * out[p]

    @pl.loop(0, PX // 4)
    def _(j):
        planes = pl.ds(j * 4, 4)
        field = th[planes].reshape(4 * NYF, NZF)
        flux = flow(1, j) * field - grad_y[planes].reshape(4 * NYF, NZF)
        high, low = split(flux)
        total = mm(mat[2], high) + mm(mat[2], low) + mm(mat[3], high)
        flux = flow(2, j) * field - grad_z[planes].reshape(4 * NYF, NZF)
        high, low = split(flux)
        total = total + mm(high, mat[0]) + mm(low, mat[0]) + mm(high, mat[1])
        grad[planes] = grad[planes] - STEP * total.reshape(4, NYF, NZF)

    for c in range(CHUNKS):
        for side in range(2):
            flux_sends[2 * c + side].wait_recv()
        rows = pl.ds(c * ROWS, ROWS)
        halo = halo_of(recv_f, c, pl.ds(0, ROWS))
        for p in range(PX):
            saved = grad[p, rows, :] + halo_term(halo, p, -STEP)
            out_saved[p, rows, :] = saved
            out_field[p, rows, :] = th[p, rows, :] + RK_B * saved

    for copy in vel_sends + theta_sends + flux_sends:
        copy.wait_send()


def drain(field, saved, out_field, out_saved, sem):
    copies = []
    for k, (src, dst) in enumerate(((field, out_field), (saved, out_saved))):
        copies.append(pltpu.make_async_copy(src, dst, sem.at[k]))
    for copy in copies:
        copy.start()
    for copy in copies:
        copy.wait()


def pin(x):
    return pltpu.with_memory_space_constraint(x, pltpu.HBM)


def solution(mesh):
    table = constants()
    block = (PX, NYF, NZF)
    whole = jax.ShapeDtypeStruct(block, F32)
    hbm = pl.BlockSpec(memory_space=pltpu.HBM)
    halo = pltpu.VMEM((2, CHUNKS, 2, ROWS, NZF), BF16)
    call = pl.pallas_call(
        kernel,
        out_shape=(whole, whole),
        in_specs=[hbm, hbm, hbm, pl.BlockSpec(memory_space=pltpu.SMEM), hbm],
        out_specs=[pl.BlockSpec(memory_space=pltpu.VMEM)] * 2,
        scratch_shapes=[
            pltpu.VMEM(block, F32),
            pltpu.VMEM(block, F32),
            pltpu.VMEM((6, 256, 256), BF16),
            pltpu.VMEM((4, 3, 96, NZF // 2), BF16),
            pltpu.VMEM(block, F32),
            pltpu.VMEM(block, F32),
            pltpu.VMEM(block, F32),
            pltpu.VMEM(block, F32),
            halo, halo, halo, halo,
            pltpu.SemaphoreType.DMA((6,)),
            pltpu.SemaphoreType.DMA((11,)),
            pltpu.SemaphoreType.DMA((11,)),
            pltpu.SemaphoreType.DMA((2, CHUNKS)),
            pltpu.SemaphoreType.DMA((2, CHUNKS)),
            pltpu.SemaphoreType.DMA((2, CHUNKS)),
            pltpu.SemaphoreType.DMA((2, CHUNKS)),
        ],
        compiler_params=pltpu.CompilerParams(
            collective_id=0, has_side_effects=True, vmem_limit_bytes=24 * 2**20
        ),
    )

    vmem = pl.BlockSpec(memory_space=pltpu.VMEM)
    store = pl.pallas_call(
        drain,
        out_shape=(whole, whole),
        in_specs=[vmem, vmem],
        out_specs=[hbm, hbm],
        scratch_shapes=[pltpu.SemaphoreType.DMA((2,))],
        compiler_params=pltpu.CompilerParams(vmem_limit_bytes=4 * 2**20),
    )

    def shards(theta, register, velocity, diffusivity):
        coarse = velocity.reshape(3, 64, NZF // 2)
        field, saved = call(
            pin(theta.reshape(block)), pin(register.reshape(block)), pin(coarse), diffusivity, pin(jnp.asarray(table))
        )
        field, saved = store(field, saved)
        return (field[None], saved[None])

    spec = P("grp", "slab", None, None)
    return jax.shard_map(
        shards, mesh=mesh,
        in_specs=(spec, spec, P(None, "slab", "grp", None), P("grp")),
        out_specs=(spec, spec), check_vma=False,
    )
```

```python
import jax
import jax.numpy as jnp
import numpy as np
from jax import lax
from jax.experimental import pallas as pl
from jax.experimental.pallas import tpu as pltpu
from jax.sharding import PartitionSpec as P

PX = 16
BLK = 32
NYF = 64
NZF = 256
ALPHA = 4.0 / 9.0
BETA = 1.0 / 36.0
COEF_A = 40.0 / 27.0
COEF_B = 25.0 / 54.0
RK_A = -5.0 / 9.0
RK_B = 15.0 / 16.0
STEP = 0.2
CHUNKS = 2
ROWS = NYF // CHUNKS
MESH = pl.DeviceIdType.MESH
F32 = jnp.float32
BF16 = jnp.bfloat16


def band(count):
    eye = lambda k: np.eye(count, k=k)
    return eye(0) + ALPHA * (eye(1) + eye(-1)) + BETA * (eye(2) + eye(-2))


def periodic_rhs(count):
    out = np.zeros((count, count))
    for i in range(count):
        for shift, weight in ((1, 0.5 * COEF_A), (2, 0.25 * COEF_B)):
            out[i, (i + shift) % count] += weight
            out[i, (i - shift) % count] -= weight
    return out


def blocked_operator(count):
    inverse = np.linalg.inv(band(BLK))
    return np.kron(np.eye(count // BLK), inverse) @ periodic_rhs(count)


def refine_matrix(count):
    out = np.zeros((2 * count, count))
    for k in range(count):
        for shift, even, odd in (
            (-2, -0.0390625, 0.0),
            (-1, 0.2734375, -0.0546875),
            (0, 0.8203125, 0.8203125),
            (1, -0.0546875, 0.2734375),
            (2, 0.0, -0.0390625),
        ):
            out[2 * k, (k + shift) % count] += even
            out[2 * k + 1, (k + shift) % count] += odd
    return out


def split_constant(matrix):
    high = jnp.asarray(matrix, F32).astype(BF16)
    rest = matrix - np.asarray(high.astype(F32), np.float64)
    return np.asarray(high), np.asarray(jnp.asarray(rest, F32).astype(BF16))


def constants():
    dz = split_constant(blocked_operator(NZF).T)
    dy = split_constant(np.kron(np.eye(4), blocked_operator(NYF)))
    ry = np.kron(np.eye(4), refine_matrix(NYF // 2))
    ry = split_constant(np.concatenate([ry, ry], axis=1))[0]
    rz = refine_matrix(NZF // 2).T
    rz = split_constant(np.concatenate([rz, rz], axis=0))[0]
    return (
        np.concatenate([dy[0], dy[0], dy[1]], axis=1),
        np.concatenate([dz[0], dz[0], dz[1]], axis=0),
        np.stack([ry, rz]),
    )


def halo_weights():
    inverse = np.linalg.inv(band(PX))
    first, second = 0.5 * COEF_A, 0.25 * COEF_B
    return np.stack(
        [
            -second * inverse[:, 0],
            -first * inverse[:, 0] - second * inverse[:, 1],
            second * inverse[:, PX - 2] + first * inverse[:, PX - 1],
            second * inverse[:, PX - 1],
        ],
        axis=1,
    )


def factors():
    lower1, lower2, diag = np.zeros(PX), np.zeros(PX), np.zeros(PX)
    for i in range(PX):
        if i >= 2:
            lower2[i] = BETA / diag[i - 2]
        if i >= 1:
            off = ALPHA - (lower2[i] * diag[i - 2] * lower1[i - 1] if i >= 2 else 0.0)
            lower1[i] = off / diag[i - 1]
        diag[i] = (
            1.0
            - (lower1[i] ** 2 * diag[i - 1] if i >= 1 else 0.0)
            - (lower2[i] ** 2 * diag[i - 2] if i >= 2 else 0.0)
        )
    return lower1, lower2, diag


WEIGHTS = halo_weights()
LOWER1, LOWER2, DIAG = factors()


def x_local(planes):
    ratio = 0.25 * COEF_B / (0.5 * COEF_A)
    scale = 0.5 * COEF_A

    def diff(i, shift):
        ahead, behind = i + shift, i - shift
        if ahead >= PX:
            return -planes[behind]
        if behind < 0:
            return planes[ahead]
        return planes[ahead] - planes[behind]

    out = []
    for i in range(PX):
        value = diff(i, 1) + ratio * diff(i, 2)
        if i >= 1:
            value = value - float(LOWER1[i]) * out[i - 1]
        if i >= 2:
            value = value - float(LOWER2[i]) * out[i - 2]
        out.append(value)
    for i in reversed(range(PX)):
        value = float(scale / DIAG[i]) * out[i]
        if i + 1 < PX:
            value = value - float(LOWER1[i + 1]) * out[i + 1]
        if i + 2 < PX:
            value = value - float(LOWER2[i + 2]) * out[i + 2]
        out[i] = value
    return out


def halo_term(halo, i, factor=1.0):
    total = float(factor * WEIGHTS[i, 0]) * halo[0]
    for k in range(1, 4):
        total = total + float(factor * WEIGHTS[i, k]) * halo[k]
    return total


def split(value):
    high = value.astype(BF16)
    return high, (value - high.astype(F32)).astype(BF16)


def mm(left, right):
    return jnp.dot(left, right, preferred_element_type=F32)


def kernel(
    theta, register, velocity, kappa, consts_y, consts_z, consts_r, out_field, out_saved,
    th, reg, mat_y, mat_z, mat_r, block, halo, grad, grad_y, grad_z, flow_x, flow_h,
    send_t, recv_t, send_g, recv_g,
    load_sem, v_send, v_recv, t_send, t_recv, g_send, g_recv,
):
    grp, slab = lax.axis_index("grp"), lax.axis_index("slab")
    count = lax.axis_size("slab")
    right, left = lax.rem(slab + 1, count), lax.rem(slab + count - 1, count)
    chip, core = lax.div(grp, 2), lax.rem(grp, 2)
    across = 1 - chip
    peer, mate = 2 * across + core, 2 * chip + 1 - core

    def load(src, dst, k):
        copy = pltpu.make_async_copy(src, dst, load_sem.at[k])
        copy.start()
        return copy

    to_peer, to_mate = {"grp": peer, "slab": slab}, {"grp": mate, "slab": slab}
    to_right, to_left = {"grp": grp, "slab": right}, {"grp": grp, "slab": left}
    far_right, far_left = {"grp": peer, "slab": right}, {"grp": peer, "slab": left}
    partners = [to_right, to_left, far_right, far_left, to_peer, to_mate]
    barrier = pltpu.get_barrier_semaphore()
    for partner in partners:
        pl.semaphore_signal(barrier, inc=1, device_id=partner, device_id_type=MESH)

    edges = [
        load(theta.at[pl.ds(0, 2)], th.at[pl.ds(0, 2)], 0),
        load(theta.at[pl.ds(PX - 2, 2)], th.at[pl.ds(PX - 2, 2)], 1),
    ]
    own_block = load(velocity, block.at[core, chip], 2)
    inner = load(theta.at[pl.ds(2, PX - 4)], th.at[pl.ds(2, PX - 4)], 3)
    load_mats = [load(consts_y, mat_y, 4), load(consts_z, mat_z, 5), load(consts_r, mat_r, 6)]
    load_reg = load(register, reg, 7)
    pl.semaphore_wait(barrier, len(partners))

    def remote(src, dst, send_sem, recv_sem, device):
        copy = pltpu.make_async_remote_copy(
            src_ref=src, dst_ref=dst, send_sem=send_sem, recv_sem=recv_sem,
            device_id=device, device_id_type=MESH,
        )
        copy.start()
        return copy

    def velocity_send(src, dst, k, device):
        return remote(src, dst, v_send.at[k], v_recv.at[k], device)

    top, bottom = velocity.at[:, pl.ds(32, 32)], velocity.at[:, pl.ds(0, 32)]
    block_send = velocity_send(velocity, block.at[core, chip], 0, to_peer)
    halo_sends = [
        velocity_send(top, halo.at[core, chip, 0], 1, to_right),
        velocity_send(bottom, halo.at[core, chip, 1], 2, to_left),
        velocity_send(top, halo.at[core, chip, 0], 3, far_right),
        velocity_send(bottom, halo.at[core, chip, 1], 4, far_left),
    ]

    for copy in edges:
        copy.wait()
    theta_sends = []
    for c in range(CHUNKS):
        rows = pl.ds(c * ROWS, ROWS)
        for side, (first, device) in enumerate(((PX - 2, to_right), (0, to_left))):
            send_t[side, c] = th[pl.ds(first, 2), rows, :].astype(BF16)
            theta_sends.append(
                remote(
                    send_t.at[side, c], recv_t.at[side, c],
                    t_send.at[side, c], t_recv.at[side, c], device,
                )
            )

    inner.wait()

    @pl.loop(0, NYF // 8)
    def _(t):
        rows = pl.ds(pl.multiple_of(t * 8, 8), 8)
        out = x_local([th[p, rows, :] for p in range(PX)])
        for p in range(PX):
            grad[p, rows, :] = out[p]

    own_block.wait()
    block_send.wait_recv()
    block_forward = velocity_send(block.at[core], block.at[core], 5, to_mate)

    for copy in load_mats:
        copy.wait()
    kap = kappa[0]

    def apply_y(value):
        high, low = split(value)
        return mm(mat_y[...], jnp.concatenate([high, low, high], axis=0))

    def apply_z(value):
        high, low = split(value)
        return mm(jnp.concatenate([high, low, high], axis=1), mat_z[...])

    def flat(value):
        return value.reshape(4 * NYF, NZF)

    def planes_of(value):
        return value.reshape(4, NYF, NZF)

    @pl.loop(0, PX // 4)
    def _(j):
        planes = pl.ds(j * 4, 4)
        value = flat(th[planes])
        grad_y[planes] = planes_of(kap * apply_y(value))
        grad_z[planes] = planes_of(kap * apply_z(value))

    def coarse_planes(comp, first, size):
        out = []
        for part in range(4):
            z, c = part // 2, part % 2
            pieces = []
            if first < 0:
                pieces.append(halo[c, z, 0, comp, pl.ds((4 + first) * 8, -first * 8), :])
            start, stop = max(first, 0), min(first + size, 8)
            pieces.append(block[c, z, comp, pl.ds(start * 8, (stop - start) * 8), :])
            if first + size > 8:
                pieces.append(halo[c, z, 1, comp, pl.ds(0, (first + size - 8) * 8), :])
            planes = [p.astype(F32).reshape(-1, 8, NZF // 2) for p in pieces]
            out.append([p[k] for p in planes for k in range(p.shape[0])])
        return out

    def even(c, k):
        return (
            -0.0390625 * c[k - 2] + 0.2734375 * c[k - 1]
            + 0.8203125 * c[k] - 0.0546875 * c[k + 1]
        )

    def odd(c, k):
        return (
            -0.0546875 * c[k - 1] + 0.8203125 * c[k]
            + 0.2734375 * c[k + 1] - 0.0390625 * c[k + 2]
        )

    def flow(tiles):
        count = len(tiles)
        stacked = jnp.concatenate([jnp.concatenate(t, axis=0) for t in tiles], axis=1)
        wide = mm(mat_r[0], jnp.concatenate(split(stacked), axis=0))
        high, low = split(wide)
        half = NZF // 2
        rows = [
            jnp.concatenate([high[:, half * k : half * k + half], low[:, half * k : half * k + half]], axis=1)
            for k in range(count)
        ]
        fine = mm(jnp.concatenate(rows, axis=0) if count > 1 else rows[0], mat_r[1])
        return [fine[256 * k : 256 * k + 256] for k in range(count)]

    def group_tiles(comp, j):
        parts = coarse_planes(comp, 2 * j - 2, 6)
        return [f(c, k) for k in (2, 3) for f in (even, odd) for c in parts]

    def edge_tiles():
        low, high = coarse_planes(0, -4, 6), coarse_planes(0, 6, 6)
        return [f(c, k) for c_set, k in ((low, 3), (high, 2)) for f in (even, odd) for c in c_set]

    def group(j, with_edges):
        planes = pl.ds(4 * j, 4)
        tiles = [group_tiles(comp, j) for comp in range(3)]
        if with_edges:
            tiles.append(edge_tiles())
        fine = flow(tiles)
        flow_x[planes] = planes_of(fine[0])
        if with_edges:
            flow_h[...] = planes_of(fine[3])
        field = flat(th[planes])
        total = apply_y(fine[1] * field - flat(grad_y[planes]))
        total = total + apply_z(fine[2] * field - flat(grad_z[planes]))
        grad_y[planes] = RK_A * reg[planes] - STEP * planes_of(total)

    load_reg.wait()
    block_forward.wait_recv()
    group(1, False)

    def halo_of(buffer, c, rows):
        return [buffer[side, c, k, rows, :].astype(F32) for side in range(2) for k in range(2)]

    grad_sends = []
    for c in range(CHUNKS):
        for side in range(2):
            theta_sends[2 * c + side].wait_recv()
        rows = pl.ds(c * ROWS, ROWS)
        near = halo_of(recv_t, c, pl.ds(0, ROWS))
        for side, (first, device) in enumerate(((PX - 2, to_right), (0, to_left))):
            for k in range(2):
                p = first + k
                value = grad[p, rows, :] + halo_term(near, p)
                send_g[side, c, k] = value.astype(BF16)
            grad_sends.append(
                remote(
                    send_g.at[side, c], recv_g.at[side, c],
                    g_send.at[side, c], g_recv.at[side, c], device,
                )
            )

    for copy in halo_sends:
        copy.wait_recv()
    halo_forward = velocity_send(halo.at[core], halo.at[core], 6, to_mate)
    group(2, False)
    halo_forward.wait_recv()
    group(0, True)
    group(3, False)

    @pl.loop(0, NYF // 16)
    def _(t):
        near = halo_of(recv_t, t * 16 // ROWS, pl.ds(pl.multiple_of(lax.rem(t * 16, ROWS), 16), 16))
        for part in range(2):
            rows = pl.ds(pl.multiple_of(t * 16 + part * 8, 8), 8)
            close = [h[part * 8 : part * 8 + 8] for h in near]
            planes = []
            for p in range(PX):
                value = grad[p, rows, :] + halo_term(close, p)
                planes.append(flow_x[p, rows, :] * th[p, rows, :] - kap * value)
            out = x_local(planes)
            for p in range(PX):
                grad_y[p, rows, :] = grad_y[p, rows, :] - STEP * out[p]

    for c in range(CHUNKS):
        for side in range(2):
            grad_sends[2 * c + side].wait_recv()

        @pl.loop(0, ROWS // 16)
        def _(t):
            near = pl.ds(pl.multiple_of(t * 16, 16), 16)
            rows = pl.ds(pl.multiple_of(c * ROWS + t * 16, 16), 16)
            slopes, fields = halo_of(recv_g, c, near), halo_of(recv_t, c, near)
            flux = [flow_h[k, rows, :] * fields[k] - kap * slopes[k] for k in range(4)]
            for p in range(PX):
                saved = grad_y[p, rows, :] + halo_term(flux, p, -STEP)
                out_saved[p, rows, :] = saved
                out_field[p, rows, :] = th[p, rows, :] + RK_B * saved

    for copy in [block_send, block_forward, halo_forward] + halo_sends + theta_sends + grad_sends:
        copy.wait_send()


def drain(field, saved, out_field, out_saved, sem):
    copies = []
    for k, (src, dst) in enumerate(((field, out_field), (saved, out_saved))):
        copies.append(pltpu.make_async_copy(src, dst, sem.at[k]))
    for copy in copies:
        copy.start()
    for copy in copies:
        copy.wait()


def pin(x):
    return pltpu.with_memory_space_constraint(x, pltpu.HBM)


def solution(mesh):
    tables = constants()
    shape = (PX, NYF, NZF)
    whole = jax.ShapeDtypeStruct(shape, F32)
    hbm = pl.BlockSpec(memory_space=pltpu.HBM)
    vmem = pl.BlockSpec(memory_space=pltpu.VMEM)
    smem = pl.BlockSpec(memory_space=pltpu.SMEM)
    edge = pltpu.VMEM((2, CHUNKS, 2, ROWS, NZF), BF16)
    dma = pltpu.SemaphoreType.DMA
    call = pl.pallas_call(
        kernel,
        out_shape=(whole, whole),
        in_specs=[hbm, hbm, hbm, smem, hbm, hbm, hbm],
        out_specs=[vmem, vmem],
        scratch_shapes=[
            pltpu.VMEM(shape, F32),
            pltpu.VMEM(shape, F32),
            pltpu.VMEM((256, 768), BF16),
            pltpu.VMEM((768, 256), BF16),
            pltpu.VMEM((2, 256, 256), BF16),
            pltpu.VMEM((2, 2, 3, 64, NZF // 2), BF16),
            pltpu.VMEM((2, 2, 2, 3, 32, NZF // 2), BF16),
            pltpu.VMEM(shape, F32),
            pltpu.VMEM(shape, F32),
            pltpu.VMEM(shape, F32),
            pltpu.VMEM(shape, F32),
            pltpu.VMEM((4, NYF, NZF), F32),
            edge, edge, edge, edge,
            dma((8,)), dma((7,)), dma((7,)),
            dma((2, CHUNKS)), dma((2, CHUNKS)), dma((2, CHUNKS)), dma((2, CHUNKS)),
        ],
        compiler_params=pltpu.CompilerParams(
            collective_id=0, has_side_effects=True, vmem_limit_bytes=24 * 2**20
        ),
    )
    store = pl.pallas_call(
        drain,
        out_shape=(whole, whole),
        in_specs=[vmem, vmem],
        out_specs=[hbm, hbm],
        scratch_shapes=[dma((2,))],
        compiler_params=pltpu.CompilerParams(vmem_limit_bytes=4 * 2**20),
    )

    def shards(theta, register, velocity, diffusivity):
        field, saved = call(
            pin(theta.reshape(shape)), pin(register.reshape(shape)),
            pin(velocity.reshape(3, 64, NZF // 2)), diffusivity,
            *[pin(jnp.asarray(table)) for table in tables],
        )
        field, saved = store(field, saved)
        return (field[None], saved[None])

    spec = P("grp", "slab", None, None)
    return jax.shard_map(
        shards, mesh=mesh,
        in_specs=(spec, spec, P(None, "slab", "grp", None), P("grp")),
        out_specs=(spec, spec), check_vma=False,
    )
```

```python
import jax
import jax.numpy as jnp
import numpy as np
from jax import lax
from jax.experimental import pallas as pl
from jax.experimental.pallas import tpu as pltpu
from jax.sharding import PartitionSpec as P

PX = 16
BLK = 32
NYF = 64
NZF = 256
ALPHA = 4.0 / 9.0
BETA = 1.0 / 36.0
COEF_A = 40.0 / 27.0
COEF_B = 25.0 / 54.0
RK_A = -5.0 / 9.0
RK_B = 15.0 / 16.0
STEP = 0.2
CHUNKS = 2
ROWS = NYF // CHUNKS
MESH = pl.DeviceIdType.MESH
F32 = jnp.float32
BF16 = jnp.bfloat16


def band(count):
    eye = lambda k: np.eye(count, k=k)
    return eye(0) + ALPHA * (eye(1) + eye(-1)) + BETA * (eye(2) + eye(-2))


def periodic_rhs(count):
    out = np.zeros((count, count))
    for i in range(count):
        for shift, weight in ((1, 0.5 * COEF_A), (2, 0.25 * COEF_B)):
            out[i, (i + shift) % count] += weight
            out[i, (i - shift) % count] -= weight
    return out


def blocked_operator(count):
    inverse = np.linalg.inv(band(BLK))
    return np.kron(np.eye(count // BLK), inverse) @ periodic_rhs(count)


def refine_matrix(count):
    out = np.zeros((2 * count, count))
    for k in range(count):
        for shift, even, odd in (
            (-2, -0.0390625, 0.0),
            (-1, 0.2734375, -0.0546875),
            (0, 0.8203125, 0.8203125),
            (1, -0.0546875, 0.2734375),
            (2, 0.0, -0.0390625),
        ):
            out[2 * k, (k + shift) % count] += even
            out[2 * k + 1, (k + shift) % count] += odd
    return out


def split_constant(matrix):
    high = jnp.asarray(matrix, F32).astype(BF16)
    rest = matrix - np.asarray(high.astype(F32), np.float64)
    return np.asarray(high), np.asarray(jnp.asarray(rest, F32).astype(BF16))


def constants():
    dz = split_constant(blocked_operator(NZF).T)
    dy = split_constant(np.kron(np.eye(4), blocked_operator(NYF)))
    ry = np.kron(np.eye(4), refine_matrix(NYF // 2))
    ry = split_constant(np.concatenate([ry, ry], axis=1))[0]
    rz = refine_matrix(NZF // 2).T
    rz = split_constant(np.concatenate([rz, rz], axis=0))[0]
    return (
        np.concatenate([dy[0], dy[0], dy[1]], axis=1),
        np.concatenate([dz[0], dz[0], dz[1]], axis=0),
        np.stack([ry, rz]),
    )


def halo_weights():
    inverse = np.linalg.inv(band(PX))
    first, second = 0.5 * COEF_A, 0.25 * COEF_B
    return np.stack(
        [
            -second * inverse[:, 0],
            -first * inverse[:, 0] - second * inverse[:, 1],
            second * inverse[:, PX - 2] + first * inverse[:, PX - 1],
            second * inverse[:, PX - 1],
        ],
        axis=1,
    )


def factors():
    lower1, lower2, diag = np.zeros(PX), np.zeros(PX), np.zeros(PX)
    for i in range(PX):
        if i >= 2:
            lower2[i] = BETA / diag[i - 2]
        if i >= 1:
            off = ALPHA - (lower2[i] * diag[i - 2] * lower1[i - 1] if i >= 2 else 0.0)
            lower1[i] = off / diag[i - 1]
        diag[i] = (
            1.0
            - (lower1[i] ** 2 * diag[i - 1] if i >= 1 else 0.0)
            - (lower2[i] ** 2 * diag[i - 2] if i >= 2 else 0.0)
        )
    return lower1, lower2, diag


WEIGHTS = halo_weights()
LOWER1, LOWER2, DIAG = factors()


def x_local(planes):
    ratio = 0.25 * COEF_B / (0.5 * COEF_A)
    scale = 0.5 * COEF_A

    def diff(i, shift):
        ahead, behind = i + shift, i - shift
        if ahead >= PX:
            return -planes[behind]
        if behind < 0:
            return planes[ahead]
        return planes[ahead] - planes[behind]

    out = []
    for i in range(PX):
        value = diff(i, 1) + ratio * diff(i, 2)
        if i >= 1:
            value = value - float(LOWER1[i]) * out[i - 1]
        if i >= 2:
            value = value - float(LOWER2[i]) * out[i - 2]
        out.append(value)
    for i in reversed(range(PX)):
        value = float(scale / DIAG[i]) * out[i]
        if i + 1 < PX:
            value = value - float(LOWER1[i + 1]) * out[i + 1]
        if i + 2 < PX:
            value = value - float(LOWER2[i + 2]) * out[i + 2]
        out[i] = value
    return out


def halo_term(halo, i, factor=1.0):
    total = float(factor * WEIGHTS[i, 0]) * halo[0]
    for k in range(1, 4):
        total = total + float(factor * WEIGHTS[i, k]) * halo[k]
    return total


def side_term(pair, i, side):
    return float(WEIGHTS[i, 2 * side]) * pair[0] + float(WEIGHTS[i, 2 * side + 1]) * pair[1]


def split(value):
    high = value.astype(BF16)
    return high, (value - high.astype(F32)).astype(BF16)


def mm(left, right):
    return jnp.dot(left, right, preferred_element_type=F32)


def kernel(
    theta, register, velocity, kappa, consts_y, consts_z, consts_r, out_field, out_saved,
    th, reg, mat_y, mat_z, mat_r, block, halo, grad, grad_y, grad_z, flow_x, flow_h,
    send_t, recv_t, send_g, recv_g,
    load_sem, v_send, v_recv, t_send, t_recv, g_send, g_recv,
):
    grp, slab = lax.axis_index("grp"), lax.axis_index("slab")
    count = lax.axis_size("slab")
    right, left = lax.rem(slab + 1, count), lax.rem(slab + count - 1, count)
    chip, core = lax.div(grp, 2), lax.rem(grp, 2)
    across = 1 - chip
    peer, mate = 2 * across + core, 2 * chip + 1 - core

    def load(src, dst, k):
        copy = pltpu.make_async_copy(src, dst, load_sem.at[k])
        copy.start()
        return copy

    to_peer, to_mate = {"grp": peer, "slab": slab}, {"grp": mate, "slab": slab}
    to_right, to_left = {"grp": grp, "slab": right}, {"grp": grp, "slab": left}
    far_right, far_left = {"grp": peer, "slab": right}, {"grp": peer, "slab": left}
    partners = [to_right, to_left, far_right, far_left, to_peer, to_mate]
    barrier = pltpu.get_barrier_semaphore()
    for partner in partners:
        pl.semaphore_signal(barrier, inc=1, device_id=partner, device_id_type=MESH)

    edges = [
        load(theta.at[pl.ds(0, 2)], th.at[pl.ds(0, 2)], 0),
        load(theta.at[pl.ds(PX - 2, 2)], th.at[pl.ds(PX - 2, 2)], 1),
    ]
    own_block = load(velocity, block.at[core, chip], 2)
    inner = load(theta.at[pl.ds(2, PX - 4)], th.at[pl.ds(2, PX - 4)], 3)
    load_mats = [load(consts_y, mat_y, 4), load(consts_z, mat_z, 5), load(consts_r, mat_r, 6)]
    load_reg = load(register, reg, 7)
    pl.semaphore_wait(barrier, len(partners))

    def remote(src, dst, send_sem, recv_sem, device):
        copy = pltpu.make_async_remote_copy(
            src_ref=src, dst_ref=dst, send_sem=send_sem, recv_sem=recv_sem,
            device_id=device, device_id_type=MESH,
        )
        copy.start()
        return copy

    def velocity_send(src, dst, k, device):
        return remote(src, dst, v_send.at[k], v_recv.at[k], device)

    top, bottom = velocity.at[:, pl.ds(32, 32)], velocity.at[:, pl.ds(0, 32)]
    block_send = velocity_send(velocity, block.at[core, chip], 0, to_peer)
    halo_sends = [
        velocity_send(top, halo.at[core, chip, 0], 1, to_right),
        velocity_send(bottom, halo.at[core, chip, 1], 2, to_left),
        velocity_send(top, halo.at[core, chip, 0], 3, far_right),
        velocity_send(bottom, halo.at[core, chip, 1], 4, far_left),
    ]

    for copy in edges:
        copy.wait()
    theta_sends = []
    for c in range(CHUNKS):
        rows = pl.ds(c * ROWS, ROWS)
        for side, (first, device) in enumerate(((PX - 2, to_right), (0, to_left))):
            send_t[side, c] = th[pl.ds(first, 2), rows, :].astype(BF16)
            theta_sends.append(
                remote(
                    send_t.at[side, c], recv_t.at[side, c],
                    t_send.at[side, c], t_recv.at[side, c], device,
                )
            )

    inner.wait()

    @pl.loop(0, NYF // 8)
    def _(t):
        rows = pl.ds(pl.multiple_of(t * 8, 8), 8)
        out = x_local([th[p, rows, :] for p in range(PX)])
        for p in range(PX):
            grad[p, rows, :] = out[p]

    own_block.wait()
    block_send.wait_recv()
    block_forward = velocity_send(block.at[core], block.at[core], 5, to_mate)

    for copy in load_mats:
        copy.wait()
    kap = kappa[0]

    def apply_y(value):
        high, low = split(value)
        return mm(mat_y[...], jnp.concatenate([high, low, high], axis=0))

    def apply_z(value):
        high, low = split(value)
        return mm(jnp.concatenate([high, low, high], axis=1), mat_z[...])

    def flat(value):
        return value.reshape(4 * NYF, NZF)

    def planes_of(value):
        return value.reshape(4, NYF, NZF)

    @pl.loop(0, PX // 4)
    def _(j):
        planes = pl.ds(j * 4, 4)
        value = flat(th[planes])
        grad_y[planes] = planes_of(kap * apply_y(value))
        grad_z[planes] = planes_of(kap * apply_z(value))

    def coarse_planes(comp, first, size):
        out = []
        for part in range(4):
            z, c = part // 2, part % 2
            pieces = []
            if first < 0:
                pieces.append(halo[c, z, 0, comp, pl.ds((4 + first) * 8, -first * 8), :])
            start, stop = max(first, 0), min(first + size, 8)
            pieces.append(block[c, z, comp, pl.ds(start * 8, (stop - start) * 8), :])
            if first + size > 8:
                pieces.append(halo[c, z, 1, comp, pl.ds(0, (first + size - 8) * 8), :])
            planes = [p.astype(F32).reshape(-1, 8, NZF // 2) for p in pieces]
            out.append([p[k] for p in planes for k in range(p.shape[0])])
        return out

    def even(c, k):
        return (
            -0.0390625 * c[k - 2] + 0.2734375 * c[k - 1]
            + 0.8203125 * c[k] - 0.0546875 * c[k + 1]
        )

    def odd(c, k):
        return (
            -0.0546875 * c[k - 1] + 0.8203125 * c[k]
            + 0.2734375 * c[k + 1] - 0.0390625 * c[k + 2]
        )

    def flow(tiles):
        count = len(tiles)
        stacked = jnp.concatenate([jnp.concatenate(t, axis=0) for t in tiles], axis=1)
        wide = mm(mat_r[0], jnp.concatenate(split(stacked), axis=0))
        high, low = split(wide)
        half = NZF // 2
        rows = [
            jnp.concatenate([high[:, half * k : half * k + half], low[:, half * k : half * k + half]], axis=1)
            for k in range(count)
        ]
        fine = mm(jnp.concatenate(rows, axis=0) if count > 1 else rows[0], mat_r[1])
        return [fine[256 * k : 256 * k + 256] for k in range(count)]

    def group_tiles(comp, j):
        parts = coarse_planes(comp, 2 * j - 2, 6)
        return [f(c, k) for k in (2, 3) for f in (even, odd) for c in parts]

    def edge_tiles():
        low, high = coarse_planes(0, -4, 6), coarse_planes(0, 6, 6)
        return [f(c, k) for c_set, k in ((low, 3), (high, 2)) for f in (even, odd) for c in c_set]

    def group(j, with_edges):
        planes = pl.ds(4 * j, 4)
        tiles = [group_tiles(comp, j) for comp in range(3)]
        if with_edges:
            tiles.append(edge_tiles())
        fine = flow(tiles)
        flow_x[planes] = planes_of(fine[0])
        if with_edges:
            flow_h[...] = planes_of(fine[3])
        field = flat(th[planes])
        total = apply_y(fine[1] * field - flat(grad_y[planes]))
        total = total + apply_z(fine[2] * field - flat(grad_z[planes]))
        grad_y[planes] = RK_A * reg[planes] - STEP * planes_of(total)

    load_reg.wait()
    block_forward.wait_recv()
    group(1, False)
    group(2, False)

    def halo_of(buffer, side, c, rows):
        return [buffer[side, c, k, rows, :].astype(F32) for k in range(2)]

    grad_sends = [[], []]
    for side, (first, device) in enumerate(((PX - 2, to_right), (0, to_left))):
        for c in range(CHUNKS):
            theta_sends[2 * c + side].wait_recv()
            rows = pl.ds(c * ROWS, ROWS)
            near = halo_of(recv_t, side, c, pl.ds(0, ROWS))
            for k in range(2):
                p = first + k
                value = grad[p, rows, :] + side_term(near, p, side)
                send_g[side, c, k] = value.astype(BF16)
            grad_sends[side].append(
                remote(
                    send_g.at[side, c], recv_g.at[side, c],
                    g_send.at[side, c], g_recv.at[side, c], device,
                )
            )

    for copy in halo_sends:
        copy.wait_recv()
    halo_forward = velocity_send(halo.at[core], halo.at[core], 6, to_mate)
    halo_forward.wait_recv()
    group(0, True)
    group(3, False)

    @pl.loop(0, NYF // 16)
    def _(t):
        at = pl.ds(pl.multiple_of(lax.rem(t * 16, ROWS), 16), 16)
        near = [h for side in range(2) for h in halo_of(recv_t, side, t * 16 // ROWS, at)]
        for part in range(2):
            rows = pl.ds(pl.multiple_of(t * 16 + part * 8, 8), 8)
            close = [h[part * 8 : part * 8 + 8] for h in near]
            planes = []
            for p in range(PX):
                value = grad[p, rows, :] + halo_term(close, p)
                planes.append(flow_x[p, rows, :] * th[p, rows, :] - kap * value)
            out = x_local(planes)
            for p in range(PX):
                grad_y[p, rows, :] = grad_y[p, rows, :] - STEP * out[p]

    for c in range(CHUNKS):
        for side in range(2):
            grad_sends[side][c].wait_recv()

        @pl.loop(0, ROWS // 16)
        def _(t):
            near = pl.ds(pl.multiple_of(t * 16, 16), 16)
            rows = pl.ds(pl.multiple_of(c * ROWS + t * 16, 16), 16)
            flux = []
            for side, (beyond, own) in enumerate(((PX - 2, 0), (0, PX - 2))):
                slopes, fields = halo_of(recv_g, side, c, near), halo_of(recv_t, side, c, near)
                mine = [th[own + k, rows, :] for k in range(2)]
                for k in range(2):
                    slope = slopes[k] + side_term(mine, beyond + k, 1 - side)
                    flux.append(flow_h[2 * side + k, rows, :] * fields[k] - kap * slope)
            for p in range(PX):
                saved = grad_y[p, rows, :] + halo_term(flux, p, -STEP)
                out_saved[p, rows, :] = saved
                out_field[p, rows, :] = th[p, rows, :] + RK_B * saved

    for copy in [block_send, block_forward, halo_forward] + halo_sends + theta_sends + grad_sends[0] + grad_sends[1]:
        copy.wait_send()


def drain(field, saved, out_field, out_saved, sem):
    copies = []
    for k, (src, dst) in enumerate(((field, out_field), (saved, out_saved))):
        copies.append(pltpu.make_async_copy(src, dst, sem.at[k]))
    for copy in copies:
        copy.start()
    for copy in copies:
        copy.wait()


def pin(x):
    return pltpu.with_memory_space_constraint(x, pltpu.HBM)


def solution(mesh):
    tables = constants()
    shape = (PX, NYF, NZF)
    whole = jax.ShapeDtypeStruct(shape, F32)
    hbm = pl.BlockSpec(memory_space=pltpu.HBM)
    vmem = pl.BlockSpec(memory_space=pltpu.VMEM)
    smem = pl.BlockSpec(memory_space=pltpu.SMEM)
    edge = pltpu.VMEM((2, CHUNKS, 2, ROWS, NZF), BF16)
    dma = pltpu.SemaphoreType.DMA
    call = pl.pallas_call(
        kernel,
        out_shape=(whole, whole),
        in_specs=[hbm, hbm, hbm, smem, hbm, hbm, hbm],
        out_specs=[vmem, vmem],
        scratch_shapes=[
            pltpu.VMEM(shape, F32),
            pltpu.VMEM(shape, F32),
            pltpu.VMEM((256, 768), BF16),
            pltpu.VMEM((768, 256), BF16),
            pltpu.VMEM((2, 256, 256), BF16),
            pltpu.VMEM((2, 2, 3, 64, NZF // 2), BF16),
            pltpu.VMEM((2, 2, 2, 3, 32, NZF // 2), BF16),
            pltpu.VMEM(shape, F32),
            pltpu.VMEM(shape, F32),
            pltpu.VMEM(shape, F32),
            pltpu.VMEM(shape, F32),
            pltpu.VMEM((4, NYF, NZF), F32),
            edge, edge, edge, edge,
            dma((8,)), dma((7,)), dma((7,)),
            dma((2, CHUNKS)), dma((2, CHUNKS)), dma((2, CHUNKS)), dma((2, CHUNKS)),
        ],
        compiler_params=pltpu.CompilerParams(
            collective_id=0, has_side_effects=True, vmem_limit_bytes=24 * 2**20
        ),
    )
    store = pl.pallas_call(
        drain,
        out_shape=(whole, whole),
        in_specs=[vmem, vmem],
        out_specs=[hbm, hbm],
        scratch_shapes=[dma((2,))],
        compiler_params=pltpu.CompilerParams(vmem_limit_bytes=4 * 2**20),
    )

    def shards(theta, register, velocity, diffusivity):
        field, saved = call(
            pin(theta.reshape(shape)), pin(register.reshape(shape)),
            pin(velocity.reshape(3, 64, NZF // 2)), diffusivity,
            *[pin(jnp.asarray(table)) for table in tables],
        )
        field, saved = store(field, saved)
        return (field[None], saved[None])

    spec = P("grp", "slab", None, None)
    return jax.shard_map(
        shards, mesh=mesh,
        in_specs=(spec, spec, P(None, "slab", "grp", None), P("grp")),
        out_specs=(spec, spec), check_vma=False,
    )
```

```python
import jax
import jax.numpy as jnp
import numpy as np
from jax import lax
from jax.experimental import pallas as pl
from jax.experimental.pallas import tpu as pltpu
from jax.sharding import PartitionSpec as P

PX = 16
BLK = 32
NYF = 64
NZF = 256
ALPHA = 4.0 / 9.0
BETA = 1.0 / 36.0
COEF_A = 40.0 / 27.0
COEF_B = 25.0 / 54.0
RK_A = -5.0 / 9.0
RK_B = 15.0 / 16.0
STEP = 0.2
CHUNKS = 2
ROWS = NYF // CHUNKS
MESH = pl.DeviceIdType.MESH
F32 = jnp.float32
BF16 = jnp.bfloat16


def band(count):
    eye = lambda k: np.eye(count, k=k)
    return eye(0) + ALPHA * (eye(1) + eye(-1)) + BETA * (eye(2) + eye(-2))


def periodic_rhs(count):
    out = np.zeros((count, count))
    for i in range(count):
        for shift, weight in ((1, 0.5 * COEF_A), (2, 0.25 * COEF_B)):
            out[i, (i + shift) % count] += weight
            out[i, (i - shift) % count] -= weight
    return out


def blocked_operator(count):
    inverse = np.linalg.inv(band(BLK))
    return np.kron(np.eye(count // BLK), inverse) @ periodic_rhs(count)


def refine_matrix(count):
    out = np.zeros((2 * count, count))
    for k in range(count):
        for shift, even, odd in (
            (-2, -0.0390625, 0.0),
            (-1, 0.2734375, -0.0546875),
            (0, 0.8203125, 0.8203125),
            (1, -0.0546875, 0.2734375),
            (2, 0.0, -0.0390625),
        ):
            out[2 * k, (k + shift) % count] += even
            out[2 * k + 1, (k + shift) % count] += odd
    return out


def split_constant(matrix):
    high = jnp.asarray(matrix, F32).astype(BF16)
    rest = matrix - np.asarray(high.astype(F32), np.float64)
    return np.asarray(high), np.asarray(jnp.asarray(rest, F32).astype(BF16))


def constants():
    dz = split_constant(blocked_operator(NZF).T)
    dy = split_constant(np.kron(np.eye(4), blocked_operator(NYF)))
    ry = np.kron(np.eye(4), refine_matrix(NYF // 2))
    ry = split_constant(np.concatenate([ry, ry], axis=1))[0]
    rz = refine_matrix(NZF // 2).T
    rz = split_constant(np.concatenate([rz, rz], axis=0))[0]
    return (
        np.concatenate([dy[0], dy[0], dy[1]], axis=1),
        np.concatenate([dz[0], dz[0], dz[1]], axis=0),
        np.stack([ry, rz]),
    )


def halo_weights():
    inverse = np.linalg.inv(band(PX))
    first, second = 0.5 * COEF_A, 0.25 * COEF_B
    return np.stack(
        [
            -second * inverse[:, 0],
            -first * inverse[:, 0] - second * inverse[:, 1],
            second * inverse[:, PX - 2] + first * inverse[:, PX - 1],
            second * inverse[:, PX - 1],
        ],
        axis=1,
    )


def factors():
    lower1, lower2, diag = np.zeros(PX), np.zeros(PX), np.zeros(PX)
    for i in range(PX):
        if i >= 2:
            lower2[i] = BETA / diag[i - 2]
        if i >= 1:
            off = ALPHA - (lower2[i] * diag[i - 2] * lower1[i - 1] if i >= 2 else 0.0)
            lower1[i] = off / diag[i - 1]
        diag[i] = (
            1.0
            - (lower1[i] ** 2 * diag[i - 1] if i >= 1 else 0.0)
            - (lower2[i] ** 2 * diag[i - 2] if i >= 2 else 0.0)
        )
    return lower1, lower2, diag


WEIGHTS = halo_weights()
LOWER1, LOWER2, DIAG = factors()


def x_local(planes):
    ratio = 0.25 * COEF_B / (0.5 * COEF_A)
    scale = 0.5 * COEF_A

    def diff(i, shift):
        ahead, behind = i + shift, i - shift
        if ahead >= PX:
            return -planes[behind]
        if behind < 0:
            return planes[ahead]
        return planes[ahead] - planes[behind]

    out = []
    for i in range(PX):
        value = diff(i, 1) + ratio * diff(i, 2)
        if i >= 1:
            value = value - float(LOWER1[i]) * out[i - 1]
        if i >= 2:
            value = value - float(LOWER2[i]) * out[i - 2]
        out.append(value)
    for i in reversed(range(PX)):
        value = float(scale / DIAG[i]) * out[i]
        if i + 1 < PX:
            value = value - float(LOWER1[i + 1]) * out[i + 1]
        if i + 2 < PX:
            value = value - float(LOWER2[i + 2]) * out[i + 2]
        out[i] = value
    return out


def halo_term(halo, i, factor=1.0):
    total = float(factor * WEIGHTS[i, 0]) * halo[0]
    for k in range(1, 4):
        total = total + float(factor * WEIGHTS[i, k]) * halo[k]
    return total


def side_term(pair, i, side):
    return float(WEIGHTS[i, 2 * side]) * pair[0] + float(WEIGHTS[i, 2 * side + 1]) * pair[1]


def split(value):
    high = value.astype(BF16)
    return high, (value - high.astype(F32)).astype(BF16)


def mm(left, right):
    return jnp.dot(left, right, preferred_element_type=F32)


def kernel(
    theta, register, velocity, kappa, consts_y, consts_z, consts_r, out_field, out_saved,
    th, reg, mat_y, mat_z, mat_r, block, halo, grad, grad_x, grad_y, grad_z, flow_x, flow_h,
    send_t, recv_t, send_g, recv_g,
    load_sem, v_send, v_recv, t_send, t_recv, g_send, g_recv,
):
    grp, slab = lax.axis_index("grp"), lax.axis_index("slab")
    count = lax.axis_size("slab")
    right, left = lax.rem(slab + 1, count), lax.rem(slab + count - 1, count)
    chip, core = lax.div(grp, 2), lax.rem(grp, 2)
    across = 1 - chip
    peer, mate = 2 * across + core, 2 * chip + 1 - core

    def load(src, dst, k):
        copy = pltpu.make_async_copy(src, dst, load_sem.at[k])
        copy.start()
        return copy

    to_peer, to_mate = {"grp": peer, "slab": slab}, {"grp": mate, "slab": slab}
    to_right, to_left = {"grp": grp, "slab": right}, {"grp": grp, "slab": left}
    far_right, far_left = {"grp": peer, "slab": right}, {"grp": peer, "slab": left}
    partners = [to_right, to_left, far_right, far_left, to_peer, to_mate]
    barrier = pltpu.get_barrier_semaphore()
    for partner in partners:
        pl.semaphore_signal(barrier, inc=1, device_id=partner, device_id_type=MESH)

    edges = [
        load(theta.at[pl.ds(0, 2)], th.at[pl.ds(0, 2)], 0),
        load(theta.at[pl.ds(PX - 2, 2)], th.at[pl.ds(PX - 2, 2)], 1),
    ]
    own_block = load(velocity, block.at[core, chip], 2)
    inner = load(theta.at[pl.ds(2, PX - 4)], th.at[pl.ds(2, PX - 4)], 3)
    load_mats = [load(consts_y, mat_y, 4), load(consts_z, mat_z, 5), load(consts_r, mat_r, 6)]
    load_reg = load(register, reg, 7)
    pl.semaphore_wait(barrier, len(partners))

    def remote(src, dst, send_sem, recv_sem, device):
        copy = pltpu.make_async_remote_copy(
            src_ref=src, dst_ref=dst, send_sem=send_sem, recv_sem=recv_sem,
            device_id=device, device_id_type=MESH,
        )
        copy.start()
        return copy

    def velocity_send(src, dst, k, device):
        return remote(src, dst, v_send.at[k], v_recv.at[k], device)

    top, bottom = velocity.at[:, pl.ds(32, 32)], velocity.at[:, pl.ds(0, 32)]
    block_send = velocity_send(velocity, block.at[core, chip], 0, to_peer)
    halo_sends = [
        velocity_send(top, halo.at[core, chip, 0], 1, to_right),
        velocity_send(bottom, halo.at[core, chip, 1], 2, to_left),
        velocity_send(top, halo.at[core, chip, 0], 3, far_right),
        velocity_send(bottom, halo.at[core, chip, 1], 4, far_left),
    ]

    for copy in edges:
        copy.wait()
    theta_sends = []
    for c in range(CHUNKS):
        rows = pl.ds(c * ROWS, ROWS)
        for side, (first, device) in enumerate(((PX - 2, to_right), (0, to_left))):
            send_t[side, c] = th[pl.ds(first, 2), rows, :].astype(BF16)
            theta_sends.append(
                remote(
                    send_t.at[side, c], recv_t.at[side, c],
                    t_send.at[side, c], t_recv.at[side, c], device,
                )
            )

    inner.wait()

    @pl.loop(0, NYF // 8)
    def _(t):
        rows = pl.ds(pl.multiple_of(t * 8, 8), 8)
        out = x_local([th[p, rows, :] for p in range(PX)])
        for p in range(PX):
            grad[p, rows, :] = out[p]

    own_block.wait()
    block_send.wait_recv()
    block_forward = velocity_send(block.at[core], block.at[core], 5, to_mate)

    for copy in load_mats:
        copy.wait()
    kap = kappa[0]

    def apply_y(value):
        high, low = split(value)
        return mm(mat_y[...], jnp.concatenate([high, low, high], axis=0))

    def apply_z(value):
        high, low = split(value)
        return mm(jnp.concatenate([high, low, high], axis=1), mat_z[...])

    def flat(value):
        return value.reshape(4 * NYF, NZF)

    def planes_of(value):
        return value.reshape(4, NYF, NZF)

    @pl.loop(0, PX // 4)
    def _(j):
        planes = pl.ds(j * 4, 4)
        value = flat(th[planes])
        grad_y[planes] = planes_of(kap * apply_y(value))
        grad_z[planes] = planes_of(kap * apply_z(value))

    def coarse_planes(comp, first, size):
        out = []
        for part in range(4):
            z, c = part // 2, part % 2
            pieces = []
            if first < 0:
                pieces.append(halo[c, z, 0, comp, pl.ds((4 + first) * 8, -first * 8), :])
            start, stop = max(first, 0), min(first + size, 8)
            pieces.append(block[c, z, comp, pl.ds(start * 8, (stop - start) * 8), :])
            if first + size > 8:
                pieces.append(halo[c, z, 1, comp, pl.ds(0, (first + size - 8) * 8), :])
            planes = [p.astype(F32).reshape(-1, 8, NZF // 2) for p in pieces]
            out.append([p[k] for p in planes for k in range(p.shape[0])])
        return out

    def even(c, k):
        return (
            -0.0390625 * c[k - 2] + 0.2734375 * c[k - 1]
            + 0.8203125 * c[k] - 0.0546875 * c[k + 1]
        )

    def odd(c, k):
        return (
            -0.0546875 * c[k - 1] + 0.8203125 * c[k]
            + 0.2734375 * c[k + 1] - 0.0390625 * c[k + 2]
        )

    def flow(tiles):
        count = len(tiles)
        stacked = jnp.concatenate([jnp.concatenate(t, axis=0) for t in tiles], axis=1)
        wide = mm(mat_r[0], jnp.concatenate(split(stacked), axis=0))
        high, low = split(wide)
        half = NZF // 2
        rows = [
            jnp.concatenate([high[:, half * k : half * k + half], low[:, half * k : half * k + half]], axis=1)
            for k in range(count)
        ]
        fine = mm(jnp.concatenate(rows, axis=0) if count > 1 else rows[0], mat_r[1])
        return [fine[256 * k : 256 * k + 256] for k in range(count)]

    def group_tiles(comp, j):
        parts = coarse_planes(comp, 2 * j - 2, 6)
        return [f(c, k) for k in (2, 3) for f in (even, odd) for c in parts]

    def edge_tiles():
        low, high = coarse_planes(0, -4, 6), coarse_planes(0, 6, 6)
        return [f(c, k) for c_set, k in ((low, 3), (high, 2)) for f in (even, odd) for c in c_set]

    def spread(j, flow_y, flow_z):
        planes = pl.ds(4 * j, 4)
        field = flat(th[planes])
        total = apply_y(flow_y * field - flat(grad_y[planes]))
        total = total + apply_z(flow_z * field - flat(grad_z[planes]))
        grad_y[planes] = RK_A * reg[planes] - STEP * planes_of(total)

    def group(j):
        fine = flow([group_tiles(comp, j) for comp in range(3)])
        flow_x[pl.ds(4 * j, 4)] = planes_of(fine[0])
        spread(j, fine[1], fine[2])

    def x_tile(t):
        rows = pl.ds(t * 8, 8)
        near = []
        for side in range(2):
            both = pl.ds((t // 2 * 16) % ROWS, 16)
            pair = halo_of(recv_t, side, t * 8 // ROWS, both)
            near += [h[t % 2 * 8 : t % 2 * 8 + 8] for h in pair]
        planes = []
        for p in range(PX):
            value = grad[p, rows, :] + halo_term(near, p)
            planes.append(flow_x[p, rows, :] * th[p, rows, :] - kap * value)
        out = x_local(planes)
        for p in range(PX):
            grad_x[p, rows, :] = out[p]

    def halo_of(buffer, side, c, rows):
        return [buffer[side, c, k, rows, :].astype(F32) for k in range(2)]

    def send_grad(side, first, device):
        sends = []
        for c in range(CHUNKS):
            theta_sends[2 * c + side].wait_recv()
            rows = pl.ds(c * ROWS, ROWS)
            near = halo_of(recv_t, side, c, pl.ds(0, ROWS))
            for k in range(2):
                p = first + k
                value = grad[p, rows, :] + side_term(near, p, side)
                send_g[side, c, k] = value.astype(BF16)
            sends.append(
                remote(
                    send_g.at[side, c], recv_g.at[side, c],
                    g_send.at[side, c], g_recv.at[side, c], device,
                )
            )
        return sends

    grad_sends = [send_grad(0, PX - 2, to_right)]
    for copy in halo_sends:
        copy.wait_recv()
    halo_forward = velocity_send(halo.at[core], halo.at[core], 6, to_mate)
    grad_sends.append(send_grad(1, 0, to_left))

    load_reg.wait()
    block_forward.wait_recv()
    group(1)
    group(2)
    halo_forward.wait_recv()

    fine = flow([group_tiles(0, 0), group_tiles(0, 3), edge_tiles()])
    flow_x[0:4] = planes_of(fine[0])
    flow_x[12:16] = planes_of(fine[1])
    flow_h[...] = planes_of(fine[2])
    for j in (0, 3):
        spread(j, *flow([group_tiles(1, j), group_tiles(2, j)]))
    for t in range(NYF // 8):
        x_tile(t)

    for c in range(CHUNKS):
        for side in range(2):
            grad_sends[side][c].wait_recv()

        @pl.loop(0, ROWS // 16)
        def _(t):
            near = pl.ds(pl.multiple_of(t * 16, 16), 16)
            rows = pl.ds(pl.multiple_of(c * ROWS + t * 16, 16), 16)
            flux = []
            for side, (beyond, own) in enumerate(((PX - 2, 0), (0, PX - 2))):
                slopes, fields = halo_of(recv_g, side, c, near), halo_of(recv_t, side, c, near)
                mine = [th[own + k, rows, :] for k in range(2)]
                for k in range(2):
                    slope = slopes[k] + side_term(mine, beyond + k, 1 - side)
                    flux.append(flow_h[2 * side + k, rows, :] * fields[k] - kap * slope)
            for p in range(PX):
                inside = grad_x[p, rows, :] + halo_term(flux, p)
                saved = grad_y[p, rows, :] - STEP * inside
                out_saved[p, rows, :] = saved
                out_field[p, rows, :] = th[p, rows, :] + RK_B * saved

    for copy in [block_send, block_forward, halo_forward] + halo_sends + theta_sends + grad_sends[0] + grad_sends[1]:
        copy.wait_send()


def drain(field, saved, out_field, out_saved, sem):
    copies = []
    for k, (src, dst) in enumerate(((field, out_field), (saved, out_saved))):
        copies.append(pltpu.make_async_copy(src, dst, sem.at[k]))
    for copy in copies:
        copy.start()
    for copy in copies:
        copy.wait()


def pin(x):
    return pltpu.with_memory_space_constraint(x, pltpu.HBM)


def solution(mesh):
    tables = constants()
    shape = (PX, NYF, NZF)
    whole = jax.ShapeDtypeStruct(shape, F32)
    hbm = pl.BlockSpec(memory_space=pltpu.HBM)
    vmem = pl.BlockSpec(memory_space=pltpu.VMEM)
    smem = pl.BlockSpec(memory_space=pltpu.SMEM)
    edge = pltpu.VMEM((2, CHUNKS, 2, ROWS, NZF), BF16)
    dma = pltpu.SemaphoreType.DMA
    call = pl.pallas_call(
        kernel,
        out_shape=(whole, whole),
        in_specs=[hbm, hbm, hbm, smem, hbm, hbm, hbm],
        out_specs=[vmem, vmem],
        scratch_shapes=[
            pltpu.VMEM(shape, F32),
            pltpu.VMEM(shape, F32),
            pltpu.VMEM((256, 768), BF16),
            pltpu.VMEM((768, 256), BF16),
            pltpu.VMEM((2, 256, 256), BF16),
            pltpu.VMEM((2, 2, 3, 64, NZF // 2), BF16),
            pltpu.VMEM((2, 2, 2, 3, 32, NZF // 2), BF16),
            pltpu.VMEM(shape, F32),
            pltpu.VMEM(shape, F32),
            pltpu.VMEM(shape, F32),
            pltpu.VMEM(shape, F32),
            pltpu.VMEM(shape, F32),
            pltpu.VMEM((4, NYF, NZF), F32),
            edge, edge, edge, edge,
            dma((8,)), dma((7,)), dma((7,)),
            dma((2, CHUNKS)), dma((2, CHUNKS)), dma((2, CHUNKS)), dma((2, CHUNKS)),
        ],
        compiler_params=pltpu.CompilerParams(
            collective_id=0, has_side_effects=True, vmem_limit_bytes=24 * 2**20
        ),
    )
    store = pl.pallas_call(
        drain,
        out_shape=(whole, whole),
        in_specs=[vmem, vmem],
        out_specs=[hbm, hbm],
        scratch_shapes=[dma((2,))],
        compiler_params=pltpu.CompilerParams(vmem_limit_bytes=4 * 2**20),
    )

    def shards(theta, register, velocity, diffusivity):
        field, saved = call(
            pin(theta.reshape(shape)), pin(register.reshape(shape)),
            pin(velocity.reshape(3, 64, NZF // 2)), diffusivity,
            *[pin(jnp.asarray(table)) for table in tables],
        )
        field, saved = store(field, saved)
        return (field[None], saved[None])

    spec = P("grp", "slab", None, None)
    return jax.shard_map(
        shards, mesh=mesh,
        in_specs=(spec, spec, P(None, "slab", "grp", None), P("grp")),
        out_specs=(spec, spec), check_vma=False,
    )
```

```python
import jax
import jax.numpy as jnp
import numpy as np
from jax import lax
from jax.experimental import pallas as pl
from jax.experimental.pallas import tpu as pltpu
from jax.sharding import PartitionSpec as P

PX = 16
BLK = 32
NYF = 64
NZF = 256
ALPHA = 4.0 / 9.0
BETA = 1.0 / 36.0
COEF_A = 40.0 / 27.0
COEF_B = 25.0 / 54.0
RK_A = -5.0 / 9.0
RK_B = 15.0 / 16.0
STEP = 0.2
CHUNKS = 2
ROWS = NYF // CHUNKS
MESH = pl.DeviceIdType.MESH
F32 = jnp.float32
BF16 = jnp.bfloat16


def band(count):
    eye = lambda k: np.eye(count, k=k)
    return eye(0) + ALPHA * (eye(1) + eye(-1)) + BETA * (eye(2) + eye(-2))


def periodic_rhs(count):
    out = np.zeros((count, count))
    for i in range(count):
        for shift, weight in ((1, 0.5 * COEF_A), (2, 0.25 * COEF_B)):
            out[i, (i + shift) % count] += weight
            out[i, (i - shift) % count] -= weight
    return out


def blocked_operator(count):
    inverse = np.linalg.inv(band(BLK))
    return np.kron(np.eye(count // BLK), inverse) @ periodic_rhs(count)


def refine_matrix(count):
    out = np.zeros((2 * count, count))
    for k in range(count):
        for shift, even, odd in (
            (-2, -0.0390625, 0.0),
            (-1, 0.2734375, -0.0546875),
            (0, 0.8203125, 0.8203125),
            (1, -0.0546875, 0.2734375),
            (2, 0.0, -0.0390625),
        ):
            out[2 * k, (k + shift) % count] += even
            out[2 * k + 1, (k + shift) % count] += odd
    return out


def split_constant(matrix):
    high = jnp.asarray(matrix, F32).astype(BF16)
    rest = matrix - np.asarray(high.astype(F32), np.float64)
    return np.asarray(high), np.asarray(jnp.asarray(rest, F32).astype(BF16))


def constants():
    dz = split_constant(blocked_operator(NZF).T)
    dy = split_constant(np.kron(np.eye(4), blocked_operator(NYF)))
    ry = np.kron(np.eye(4), refine_matrix(NYF // 2))
    ry = split_constant(np.concatenate([ry, ry], axis=1))[0]
    rz = refine_matrix(NZF // 2).T
    rz = split_constant(np.concatenate([rz, rz], axis=0))[0]
    return (
        np.concatenate([dy[0], dy[0], dy[1]], axis=1),
        np.concatenate([dz[0], dz[0], dz[1]], axis=0),
        np.stack([ry, rz]),
    )


def halo_weights():
    inverse = np.linalg.inv(band(PX))
    first, second = 0.5 * COEF_A, 0.25 * COEF_B
    return np.stack(
        [
            -second * inverse[:, 0],
            -first * inverse[:, 0] - second * inverse[:, 1],
            second * inverse[:, PX - 2] + first * inverse[:, PX - 1],
            second * inverse[:, PX - 1],
        ],
        axis=1,
    )


def factors():
    lower1, lower2, diag = np.zeros(PX), np.zeros(PX), np.zeros(PX)
    for i in range(PX):
        if i >= 2:
            lower2[i] = BETA / diag[i - 2]
        if i >= 1:
            off = ALPHA - (lower2[i] * diag[i - 2] * lower1[i - 1] if i >= 2 else 0.0)
            lower1[i] = off / diag[i - 1]
        diag[i] = (
            1.0
            - (lower1[i] ** 2 * diag[i - 1] if i >= 1 else 0.0)
            - (lower2[i] ** 2 * diag[i - 2] if i >= 2 else 0.0)
        )
    return lower1, lower2, diag


WEIGHTS = halo_weights()
LOWER1, LOWER2, DIAG = factors()


def x_local(planes):
    ratio = 0.25 * COEF_B / (0.5 * COEF_A)
    scale = 0.5 * COEF_A

    def diff(i, shift):
        ahead, behind = i + shift, i - shift
        if ahead >= PX:
            return -planes[behind]
        if behind < 0:
            return planes[ahead]
        return planes[ahead] - planes[behind]

    out = []
    for i in range(PX):
        value = diff(i, 1) + ratio * diff(i, 2)
        if i >= 1:
            value = value - float(LOWER1[i]) * out[i - 1]
        if i >= 2:
            value = value - float(LOWER2[i]) * out[i - 2]
        out.append(value)
    for i in reversed(range(PX)):
        value = float(scale / DIAG[i]) * out[i]
        if i + 1 < PX:
            value = value - float(LOWER1[i + 1]) * out[i + 1]
        if i + 2 < PX:
            value = value - float(LOWER2[i + 2]) * out[i + 2]
        out[i] = value
    return out


def halo_term(halo, i, factor=1.0):
    total = float(factor * WEIGHTS[i, 0]) * halo[0]
    for k in range(1, 4):
        total = total + float(factor * WEIGHTS[i, k]) * halo[k]
    return total


def side_term(pair, i, side):
    return float(WEIGHTS[i, 2 * side]) * pair[0] + float(WEIGHTS[i, 2 * side + 1]) * pair[1]


def split(value):
    high = value.astype(BF16)
    return high, (value - high.astype(F32)).astype(BF16)


def mm(left, right):
    return jnp.dot(left, right, preferred_element_type=F32)


def kernel(
    theta, register, velocity, kappa, consts_y, consts_z, consts_r, out_field, out_saved,
    th, reg, mat_y, mat_z, mat_r, block, halo, grad, grad_x, grad_y, grad_z, flow_x, flow_h,
    send_t, recv_t, send_g, recv_g,
    load_sem, v_send, v_recv, t_send, t_recv, g_send, g_recv,
):
    grp, slab = lax.axis_index("grp"), lax.axis_index("slab")
    count = lax.axis_size("slab")
    right, left = lax.rem(slab + 1, count), lax.rem(slab + count - 1, count)
    chip, core = lax.div(grp, 2), lax.rem(grp, 2)
    across = 1 - chip
    peer, mate = 2 * across + core, 2 * chip + 1 - core

    def load(src, dst, k):
        copy = pltpu.make_async_copy(src, dst, load_sem.at[k])
        copy.start()
        return copy

    to_peer, to_mate = {"grp": peer, "slab": slab}, {"grp": mate, "slab": slab}
    to_right, to_left = {"grp": grp, "slab": right}, {"grp": grp, "slab": left}
    far_right, far_left = {"grp": peer, "slab": right}, {"grp": peer, "slab": left}
    partners = [to_right, to_left, far_right, far_left, to_peer, to_mate]
    barrier = pltpu.get_barrier_semaphore()
    for partner in partners:
        pl.semaphore_signal(barrier, inc=1, device_id=partner, device_id_type=MESH)

    edges = [
        load(theta.at[pl.ds(0, 2)], th.at[pl.ds(0, 2)], 0),
        load(theta.at[pl.ds(PX - 2, 2)], th.at[pl.ds(PX - 2, 2)], 1),
    ]
    own_block = load(velocity, block.at[core, chip], 2)
    inner = load(theta.at[pl.ds(2, PX - 4)], th.at[pl.ds(2, PX - 4)], 3)
    load_mats = [load(consts_y, mat_y, 4), load(consts_z, mat_z, 5), load(consts_r, mat_r, 6)]
    load_reg = load(register, reg, 7)
    pl.semaphore_wait(barrier, len(partners))

    def remote(src, dst, send_sem, recv_sem, device):
        copy = pltpu.make_async_remote_copy(
            src_ref=src, dst_ref=dst, send_sem=send_sem, recv_sem=recv_sem,
            device_id=device, device_id_type=MESH,
        )
        copy.start()
        return copy

    def velocity_send(src, dst, k, device):
        return remote(src, dst, v_send.at[k], v_recv.at[k], device)

    top, bottom = velocity.at[:, pl.ds(32, 32)], velocity.at[:, pl.ds(0, 32)]
    halo_sends = [
        velocity_send(top, halo.at[core, chip, 0], 1, to_right),
        velocity_send(bottom, halo.at[core, chip, 1], 2, to_left),
        velocity_send(top, halo.at[core, chip, 0], 3, far_right),
        velocity_send(bottom, halo.at[core, chip, 1], 4, far_left),
    ]

    for copy in edges:
        copy.wait()
    theta_sends = []
    for c in range(CHUNKS):
        rows = pl.ds(c * ROWS, ROWS)
        for side, (first, device) in enumerate(((PX - 2, to_right), (0, to_left))):
            send_t[side, c] = th[pl.ds(first, 2), rows, :].astype(BF16)
            theta_sends.append(
                remote(
                    send_t.at[side, c], recv_t.at[side, c],
                    t_send.at[side, c], t_recv.at[side, c], device,
                )
            )

    block_send = velocity_send(velocity, block.at[core, chip], 0, to_peer)
    inner.wait()

    @pl.loop(0, NYF // 8)
    def _(t):
        rows = pl.ds(pl.multiple_of(t * 8, 8), 8)
        out = x_local([th[p, rows, :] for p in range(PX)])
        for p in range(PX):
            grad[p, rows, :] = out[p]

    for copy in load_mats:
        copy.wait()
    kap = kappa[0]

    def apply_y(value):
        high, low = split(value)
        return mm(mat_y[...], jnp.concatenate([high, low, high], axis=0))

    def apply_z(value):
        high, low = split(value)
        return mm(jnp.concatenate([high, low, high], axis=1), mat_z[...])

    def flat(value):
        return value.reshape(4 * NYF, NZF)

    def planes_of(value):
        return value.reshape(4, NYF, NZF)

    @pl.loop(0, PX // 4)
    def _(j):
        planes = pl.ds(j * 4, 4)
        value = flat(th[planes])
        grad_y[planes] = planes_of(kap * apply_y(value))
        grad_z[planes] = planes_of(kap * apply_z(value))

    own_block.wait()
    block_send.wait_recv()
    block_forward = velocity_send(block.at[core], block.at[core], 5, to_mate)

    def coarse_planes(comp, first, size):
        out = []
        for part in range(4):
            z, c = part // 2, part % 2
            pieces = []
            if first < 0:
                pieces.append(halo[c, z, 0, comp, pl.ds((4 + first) * 8, -first * 8), :])
            start, stop = max(first, 0), min(first + size, 8)
            pieces.append(block[c, z, comp, pl.ds(start * 8, (stop - start) * 8), :])
            if first + size > 8:
                pieces.append(halo[c, z, 1, comp, pl.ds(0, (first + size - 8) * 8), :])
            planes = [p.astype(F32).reshape(-1, 8, NZF // 2) for p in pieces]
            out.append([p[k] for p in planes for k in range(p.shape[0])])
        return out

    def even(c, k):
        return (
            -0.0390625 * c[k - 2] + 0.2734375 * c[k - 1]
            + 0.8203125 * c[k] - 0.0546875 * c[k + 1]
        )

    def odd(c, k):
        return (
            -0.0546875 * c[k - 1] + 0.8203125 * c[k]
            + 0.2734375 * c[k + 1] - 0.0390625 * c[k + 2]
        )

    def flow(tiles):
        count = len(tiles)
        stacked = jnp.concatenate([jnp.concatenate(t, axis=0) for t in tiles], axis=1)
        wide = mm(mat_r[0], jnp.concatenate(split(stacked), axis=0))
        high, low = split(wide)
        half = NZF // 2
        rows = [
            jnp.concatenate([high[:, half * k : half * k + half], low[:, half * k : half * k + half]], axis=1)
            for k in range(count)
        ]
        fine = mm(jnp.concatenate(rows, axis=0) if count > 1 else rows[0], mat_r[1])
        return [fine[256 * k : 256 * k + 256] for k in range(count)]

    def group_tiles(comp, j):
        parts = coarse_planes(comp, 2 * j - 2, 6)
        return [f(c, k) for k in (2, 3) for f in (even, odd) for c in parts]

    def edge_tiles():
        low, high = coarse_planes(0, -4, 6), coarse_planes(0, 6, 6)
        return [f(c, k) for c_set, k in ((low, 3), (high, 2)) for f in (even, odd) for c in c_set]

    def spread(j, flow_y, flow_z):
        planes = pl.ds(4 * j, 4)
        field = flat(th[planes])
        total = apply_y(flow_y * field - flat(grad_y[planes]))
        total = total + apply_z(flow_z * field - flat(grad_z[planes]))
        grad_y[planes] = RK_A * reg[planes] - STEP * planes_of(total)

    def group(j):
        fine = flow([group_tiles(comp, j) for comp in range(3)])
        flow_x[pl.ds(4 * j, 4)] = planes_of(fine[0])
        spread(j, fine[1], fine[2])

    def x_tile(t):
        rows = pl.ds(t * 8, 8)
        near = []
        for side in range(2):
            both = pl.ds((t // 2 * 16) % ROWS, 16)
            pair = halo_of(recv_t, side, t * 8 // ROWS, both)
            near += [h[t % 2 * 8 : t % 2 * 8 + 8] for h in pair]
        planes = []
        for p in range(PX):
            value = grad[p, rows, :] + halo_term(near, p)
            planes.append(flow_x[p, rows, :] * th[p, rows, :] - kap * value)
        out = x_local(planes)
        for p in range(PX):
            grad_x[p, rows, :] = out[p]

    def halo_of(buffer, side, c, rows):
        return [buffer[side, c, k, rows, :].astype(F32) for k in range(2)]

    def send_grad(side, first, device):
        sends = []
        for c in range(CHUNKS):
            theta_sends[2 * c + side].wait_recv()
            rows = pl.ds(c * ROWS, ROWS)
            near = halo_of(recv_t, side, c, pl.ds(0, ROWS))
            for k in range(2):
                p = first + k
                value = grad[p, rows, :] + side_term(near, p, side)
                send_g[side, c, k] = value.astype(BF16)
            sends.append(
                remote(
                    send_g.at[side, c], recv_g.at[side, c],
                    g_send.at[side, c], g_recv.at[side, c], device,
                )
            )
        return sends

    grad_sends = [send_grad(0, PX - 2, to_right)]
    for copy in halo_sends:
        copy.wait_recv()
    halo_forward = velocity_send(halo.at[core], halo.at[core], 6, to_mate)
    grad_sends.append(send_grad(1, 0, to_left))

    load_reg.wait()
    block_forward.wait_recv()
    group(1)
    group(2)
    halo_forward.wait_recv()

    fine = flow([group_tiles(0, 0), group_tiles(0, 3), edge_tiles()])
    flow_x[0:4] = planes_of(fine[0])
    flow_x[12:16] = planes_of(fine[1])
    flow_h[...] = planes_of(fine[2])
    for j in (0, 3):
        spread(j, *flow([group_tiles(1, j), group_tiles(2, j)]))
    for t in range(NYF // 8):
        x_tile(t)

    for c in range(CHUNKS):
        for side in range(2):
            grad_sends[side][c].wait_recv()

        @pl.loop(0, ROWS // 16)
        def _(t):
            near = pl.ds(pl.multiple_of(t * 16, 16), 16)
            rows = pl.ds(pl.multiple_of(c * ROWS + t * 16, 16), 16)
            flux = []
            for side, (beyond, own) in enumerate(((PX - 2, 0), (0, PX - 2))):
                slopes, fields = halo_of(recv_g, side, c, near), halo_of(recv_t, side, c, near)
                mine = [th[own + k, rows, :] for k in range(2)]
                for k in range(2):
                    slope = slopes[k] + side_term(mine, beyond + k, 1 - side)
                    flux.append(flow_h[2 * side + k, rows, :] * fields[k] - kap * slope)
            for p in range(PX):
                inside = grad_x[p, rows, :] + halo_term(flux, p)
                saved = grad_y[p, rows, :] - STEP * inside
                out_saved[p, rows, :] = saved
                out_field[p, rows, :] = th[p, rows, :] + RK_B * saved

    for copy in [block_send, block_forward, halo_forward] + halo_sends + theta_sends + grad_sends[0] + grad_sends[1]:
        copy.wait_send()


def drain(field, saved, out_field, out_saved, sem):
    copies = []
    for k, (src, dst) in enumerate(((field, out_field), (saved, out_saved))):
        copies.append(pltpu.make_async_copy(src, dst, sem.at[k]))
    for copy in copies:
        copy.start()
    for copy in copies:
        copy.wait()


def pin(x):
    return pltpu.with_memory_space_constraint(x, pltpu.HBM)


def solution(mesh):
    tables = constants()
    shape = (PX, NYF, NZF)
    whole = jax.ShapeDtypeStruct(shape, F32)
    hbm = pl.BlockSpec(memory_space=pltpu.HBM)
    vmem = pl.BlockSpec(memory_space=pltpu.VMEM)
    smem = pl.BlockSpec(memory_space=pltpu.SMEM)
    edge = pltpu.VMEM((2, CHUNKS, 2, ROWS, NZF), BF16)
    dma = pltpu.SemaphoreType.DMA
    call = pl.pallas_call(
        kernel,
        out_shape=(whole, whole),
        in_specs=[hbm, hbm, hbm, smem, hbm, hbm, hbm],
        out_specs=[vmem, vmem],
        scratch_shapes=[
            pltpu.VMEM(shape, F32),
            pltpu.VMEM(shape, F32),
            pltpu.VMEM((256, 768), BF16),
            pltpu.VMEM((768, 256), BF16),
            pltpu.VMEM((2, 256, 256), BF16),
            pltpu.VMEM((2, 2, 3, 64, NZF // 2), BF16),
            pltpu.VMEM((2, 2, 2, 3, 32, NZF // 2), BF16),
            pltpu.VMEM(shape, F32),
            pltpu.VMEM(shape, F32),
            pltpu.VMEM(shape, F32),
            pltpu.VMEM(shape, F32),
            pltpu.VMEM(shape, F32),
            pltpu.VMEM((4, NYF, NZF), F32),
            edge, edge, edge, edge,
            dma((8,)), dma((7,)), dma((7,)),
            dma((2, CHUNKS)), dma((2, CHUNKS)), dma((2, CHUNKS)), dma((2, CHUNKS)),
        ],
        compiler_params=pltpu.CompilerParams(
            collective_id=0, has_side_effects=True, vmem_limit_bytes=24 * 2**20
        ),
    )
    store = pl.pallas_call(
        drain,
        out_shape=(whole, whole),
        in_specs=[vmem, vmem],
        out_specs=[hbm, hbm],
        scratch_shapes=[dma((2,))],
        compiler_params=pltpu.CompilerParams(vmem_limit_bytes=4 * 2**20),
    )

    def shards(theta, register, velocity, diffusivity):
        field, saved = call(
            pin(theta.reshape(shape)), pin(register.reshape(shape)),
            pin(velocity.reshape(3, 64, NZF // 2)), diffusivity,
            *[pin(jnp.asarray(table)) for table in tables],
        )
        field, saved = store(field, saved)
        return (field[None], saved[None])

    spec = P("grp", "slab", None, None)
    return jax.shard_map(
        shards, mesh=mesh,
        in_specs=(spec, spec, P(None, "slab", "grp", None), P("grp")),
        out_specs=(spec, spec), check_vma=False,
    )
```
